32 devices in a mesh: rows: 4 (over z), cols: 8 (over y, x, core).
Axes of the slice: x: 2, y: 2, z: 4, core: 2. Of those that a mesh axis runs over, the one named last changes fastest.
Arguments:
- blocks: bfloat16 [4, 8, 32, 256, 256], P('rows', 'cols'), may hold values from -600 to 600
- block_row: int32 [4, 8, 32], P('rows', 'cols'), may hold values from 0 to 15, as said below
- block_col: int32 [4, 8, 32], P('rows', 'cols'), may hold values from 0 to 15, as said below
- objective: float32 [32768, 48], P(('cols', 'rows')), may hold values from -3600 to 3600
- demand: float32 [16384, 48], P(('rows', 'cols')), may hold values from -2560 to 2560
- capacity: float32 [32768, 48], P(('cols', 'rows')), may hold values from 0.02 to 0.5
- step_size: float32 [3, 48], replicated, may hold values from 0.0055242716 to 0.011048543
- restart: int32 [3, 48], replicated, may hold values from 0 to 1
- primal_weight: float32 [48], replicated, may hold values from 0.5 to 2
Outputs:
- primal_flow: float32 [32768, 48], P(('cols', 'rows'))
- dual_prices: float32 [16384, 48], P(('rows', 'cols'))
- final_weight: float32 [48], replicated
The draws below stay inside these ranges and needn't reach their ends.
Inputs may be any that keep to these rules, and one draw needn't show every extreme that they name: `block_row`: on each device the 32 blocks sit in distinct slots (block row, block column), listed in increasing order of block row * 16 + block column; every block row of a row group and every block column of a column group holds a block on every device. `block_col`: goes with block_row, as described there.
All inputs are finite; a program needn't handle non-finite values.
Results may differ from the reference program's by a relative error of at most 0.00097.
Values may be sent and summed in bfloat16 or wider, within the bound.
No kernel may reach another device: no remote copies, remote signals or barrier semaphores. Data moves between devices by JAX's collectives and lax.ppermute only.
A program may use at most 64 MiB of HBM per device.

```python
import math
import jax
import jax.numpy as jnp
from jax import lax

BLK = 256
RB = 16
CB = 16
NB = 32
S = 48
PASSES = 3
ITERS = 3
ROWS_ALL = 16384
COLS_ALL = 32768
N_ROWS = 4
N_COLS = 8


def block_slots(key):
    keys = jax.random.split(key, N_ROWS * N_COLS)
    slot_ids = jnp.arange(RB * CB, dtype=jnp.int32)
    anchored = slot_ids % CB == slot_ids // CB % CB

    def one_device(device_key):
        shuffled = jax.random.permutation(device_key, RB * CB).astype(jnp.int32)
        priority = jnp.where(anchored, shuffled - RB * CB, shuffled)
        chosen = jnp.argsort(priority, stable=True)[:NB]
        return jnp.sort(chosen).astype(jnp.int32)
    return jax.vmap(one_device)(keys).reshape(N_ROWS, N_COLS, NB)


def draw_block_row(key, part):
    return (block_slots(key) // CB).astype(jnp.int32)


def draw_block_col(key, part):
    return (block_slots(key) % CB).astype(jnp.int32)


def draw_blocks(key, part):
    slots = block_slots(key)
    key = jax.random.fold_in(key, 11)
    first_key, second_key, third_key = jax.random.split(key, 3)
    spread = math.log(10.0)
    row_factor = jnp.exp(jax.random.uniform(first_key, (N_ROWS * RB * BLK,), jnp.float32) * spread)
    col_factor = jnp.exp(jax.random.uniform(second_key, (N_COLS * CB * BLK,), jnp.float32) * spread)
    rows_of = slots // CB
    cols_of = slots % CB
    row_pick = row_factor.reshape(N_ROWS, RB, BLK)[jnp.arange(N_ROWS)[:, None, None], rows_of]
    col_pick = col_factor.reshape(N_COLS, CB, BLK)[jnp.arange(N_COLS)[None, :, None], cols_of]
    shape = (N_ROWS, N_COLS, NB, BLK, BLK)
    noise = jnp.clip(jax.random.normal(third_key, shape, jnp.float32), -6.0, 6.0)
    return (noise * row_pick[:, :, :, :, None] * col_pick[:, :, :, None, :]).astype(jnp.bfloat16)


def draw_objective(key, part):
    key = jax.random.fold_in(key, 5)
    count = N_COLS * CB * BLK
    ramp = 1.0 + 2.0 * jnp.arange(count, dtype=jnp.float32) / (count - 1)
    noise = jnp.clip(jax.random.normal(key, (count, S), jnp.float32), -6.0, 6.0)
    return (200.0 * noise * ramp[:, None]).astype(jnp.float32)


def place_ends(result, rng, least, high):
    longest = result.shape.index(max(result.shape))
    spots = []
    for shift in (0, 1):
        where = [jax.random.randint(jax.random.fold_in(rng, axis), (), 0, length) for axis, length in enumerate(result.shape)]
        where[longest] = (where[longest] + shift) % result.shape[longest]
        spots.append(tuple(where))
    return result.at[spots[0]].set(least).at[spots[1]].set(high)


def block_levels(stream_key, shape, cuts, low, top_value):
    gain = 1.0
    for position, blocks in cuts:
        draws = jax.random.uniform(jax.random.fold_in(jax.random.fold_in(stream_key, 6), position), (blocks,), jnp.float32, low / len(cuts), top_value / len(cuts))
        gain = gain * jnp.repeat(jnp.exp(draws), shape[position] // blocks).reshape((-1,) + (1,) * (len(shape) - 1 - position))
    return gain


def scatter_about(stream_key, shape, scale, most, cuts=(), held_as=jnp.bfloat16):
    array = scale * jax.random.normal(stream_key, shape, jnp.float32)
    if cuts:
        array = array * block_levels(stream_key, shape, cuts, -0.22, 0.18)
    return jnp.clip(array, -most, most).astype(held_as)


def setup_inputs(seed: int = 0) -> dict:
    arg_keys = jax.random.split(jax.random.key(seed), 10)
    blocks = draw_blocks(jax.random.fold_in(arg_keys[9], 71), 0)
    block_row = draw_block_row(jax.random.fold_in(arg_keys[9], 71), 0)
    block_col = draw_block_col(jax.random.fold_in(arg_keys[9], 71), 0)
    objective = draw_objective(jax.random.fold_in(arg_keys[9], 71), 0)
    demand = scatter_about(arg_keys[4], (ROWS_ALL, S), 400.0, 2560.0, ((0, 32),), jnp.float32)
    capacity = jnp.clip(jnp.exp(math.log(0.5) - 3.218876 * jax.random.uniform(arg_keys[5], (COLS_ALL, S), jnp.float32) ** block_levels(arg_keys[5], (COLS_ALL, S), ((0, 32),), -0.2, 0.2)), 0.02, 0.5)
    step_size = jnp.clip(jnp.exp(jax.random.uniform(arg_keys[6], (ITERS, S), jnp.float32, math.log(0.0055242716), math.log(0.011048543))), 0.0055242716, 0.011048543)
    restart = place_ends(jax.random.randint(arg_keys[7], (ITERS, S), 0, 2), jax.random.fold_in(arg_keys[7], 1), 0, 1).astype(jnp.int32)
    primal_weight = jnp.clip(jnp.exp(jax.random.uniform(arg_keys[8], (S,), jnp.float32, math.log(0.5), math.log(2.0))), 0.5, 2.0)
    return {"blocks": blocks, "block_row": block_row, "block_col": block_col, "objective": objective, "demand": demand, "capacity": capacity, "step_size": step_size, "restart": restart, "primal_weight": primal_weight}


epsilon = 1e-06

def scale_blocks(matrix, row_factor, col_factor):
    return matrix.astype(jnp.float32) * row_factor[:, :, None] * col_factor[:, None, :]

def extreme_parts(scaled, rows_of, cols_of):
    magnitude = jnp.abs(scaled)
    row_hot = rows_of[:, None] == jnp.arange(RB)[None, :]
    col_hot = cols_of[:, None] == jnp.arange(CB)[None, :]
    row_part = lax.optimization_barrier(jnp.max(jnp.where(row_hot[:, :, None], lax.optimization_barrier(jnp.max(magnitude, axis=2))[:, None, :], 0.0), axis=0))
    col_part = lax.optimization_barrier(jnp.max(jnp.where(col_hot[:, :, None], lax.optimization_barrier(jnp.max(magnitude, axis=1))[:, None, :], 0.0), axis=0))
    return (row_part.reshape(RB * BLK), col_part.reshape(CB * BLK))

def device_matrix(blocks, row_scale, col_scale, block_row, block_col, row_group, col_group):
    rows_here = row_scale.reshape(N_ROWS, RB, BLK)[row_group][block_row[row_group, col_group]]
    cols_here = col_scale.reshape(N_COLS, CB, BLK)[col_group][block_col[row_group, col_group]]
    return scale_blocks(blocks[row_group, col_group], rows_here, cols_here)

def reference(blocks, block_row, block_col, objective, demand, capacity, step_size, restart, primal_weight):
    highest = lax.Precision.HIGHEST
    row_scale = jnp.ones((N_ROWS * RB * BLK,), jnp.float32)
    col_scale = jnp.ones((N_COLS * CB * BLK,), jnp.float32)
    devices = jnp.arange(N_ROWS * N_COLS, dtype=jnp.int32)
    for sweep in range(PASSES):

        def device_max(device):
            row_group = device // N_COLS
            col_group = device % N_COLS
            scaled = device_matrix(blocks, row_scale, col_scale, block_row, block_col, row_group, col_group)
            return extreme_parts(scaled, block_row[row_group, col_group], block_col[row_group, col_group])
        row_parts, col_parts = lax.map(device_max, devices)
        row_max = lax.optimization_barrier(jnp.max(row_parts.reshape(N_ROWS, N_COLS, RB * BLK), axis=1)).reshape(-1)
        col_max = lax.optimization_barrier(jnp.max(col_parts.reshape(N_ROWS, N_COLS, CB * BLK), axis=0)).reshape(-1)
        row_scale = row_scale / jnp.sqrt(row_max + epsilon)
        col_scale = col_scale / jnp.sqrt(col_max + epsilon)

    def forward(primal_bar):

        def per_group(row_group):

            def accumulate(total, col_group):
                matrix = device_matrix(blocks, row_scale, col_scale, block_row, block_col, row_group, col_group).astype(jnp.bfloat16)
                picked = primal_bar.reshape(N_COLS, CB, BLK, S)[col_group][block_col[row_group, col_group]]
                products = jnp.einsum('nij,njs->nis', matrix.astype(jnp.float32), picked.astype(jnp.float32), precision=highest)
                row_hot = (block_row[row_group, col_group][:, None] == jnp.arange(RB)[None, :]).astype(jnp.float32)
                return (total + jnp.einsum('nr,nis->ris', row_hot, products, precision=highest), None)
            total, unused = lax.scan(accumulate, jnp.zeros((RB, BLK, S), jnp.float32), jnp.arange(N_COLS, dtype=jnp.int32))
            return total.reshape(RB * BLK, S)
        return lax.map(per_group, jnp.arange(N_ROWS, dtype=jnp.int32)).reshape(N_ROWS * RB * BLK, S)

    def backward(dual_bar):

        def per_group(col_group):

            def accumulate(total, row_group):
                matrix = device_matrix(blocks, row_scale, col_scale, block_row, block_col, row_group, col_group).astype(jnp.bfloat16)
                picked = dual_bar.reshape(N_ROWS, RB, BLK, S)[row_group][block_row[row_group, col_group]]
                products = jnp.einsum('nij,nis->njs', matrix.astype(jnp.float32), picked.astype(jnp.float32), precision=highest)
                col_hot = (block_col[row_group, col_group][:, None] == jnp.arange(CB)[None, :]).astype(jnp.float32)
                return (total + jnp.einsum('nc,njs->cjs', col_hot, products, precision=highest), None)
            total, unused = lax.scan(accumulate, jnp.zeros((CB, BLK, S), jnp.float32), jnp.arange(N_ROWS, dtype=jnp.int32))
            return total.reshape(CB * BLK, S)
        return lax.map(per_group, jnp.arange(N_COLS, dtype=jnp.int32)).reshape(N_COLS * CB * BLK, S)
    scaled_cost = objective * col_scale[:, None]
    scaled_demand = demand * row_scale[:, None]
    upper = capacity / col_scale[:, None]
    primal = jnp.zeros((N_COLS * CB * BLK, S), jnp.float32)
    dual = jnp.zeros((N_ROWS * RB * BLK, S), jnp.float32)
    anchor_primal = primal
    anchor_dual = dual
    sum_primal = primal
    sum_dual = dual
    weight_total = jnp.zeros((S,), jnp.float32)
    weight = primal_weight
    for iteration in range(ITERS):
        stride = step_size[iteration]
        primal_step = stride / weight
        dual_step = stride * weight
        if iteration == 0:
            gradient = scaled_cost
        else:
            gradient = scaled_cost - backward(dual.astype(jnp.bfloat16))
        new_primal = jnp.clip(primal - primal_step[None, :] * gradient, 0.0, upper)
        extrapolated = (2.0 * new_primal - primal).astype(jnp.bfloat16)
        image = forward(extrapolated)
        dual = dual + dual_step[None, :] * (scaled_demand - image)
        primal = new_primal
        sum_primal = sum_primal + stride[None, :] * primal
        sum_dual = sum_dual + stride[None, :] * dual
        weight_total = weight_total + stride
        mean_primal = sum_primal / weight_total[None, :]
        mean_dual = sum_dual / weight_total[None, :]
        primal_move = mean_primal - anchor_primal
        dual_move = mean_dual - anchor_dual
        drift_primal = lax.optimization_barrier(jnp.sum(primal_move * primal_move, axis=0))
        drift_dual = lax.optimization_barrier(jnp.sum(dual_move * dual_move, axis=0))
        candidate = jnp.sqrt(weight * jnp.sqrt((drift_dual + epsilon) / (drift_primal + epsilon)))
        restart_now = restart[iteration] == 1
        weight = jnp.where(restart_now, candidate, weight)
        primal = jnp.where(restart_now[None, :], mean_primal, primal)
        dual = jnp.where(restart_now[None, :], mean_dual, dual)
        anchor_primal = jnp.where(restart_now[None, :], mean_primal, anchor_primal)
        anchor_dual = jnp.where(restart_now[None, :], mean_dual, anchor_dual)
        sum_primal = jnp.where(restart_now[None, :], 0.0, sum_primal)
        sum_dual = jnp.where(restart_now[None, :], 0.0, sum_dual)
        weight_total = jnp.where(restart_now, 0.0, weight_total)
    return (primal, dual, weight)
```

```python
import functools

import jax
import jax.numpy as jnp
from jax import lax
from jax.experimental import pallas as pl
from jax.experimental.pallas import tpu as pltpu
from jax.sharding import PartitionSpec as P

BLK = 256
RB = 16
CB = 16
PASSES = 3
ITERS = 3
LANES = 128
CHUNKS = 8

epsilon = 1e-06
F32 = jnp.float32
BF16 = jnp.bfloat16
VMEM = pl.BlockSpec(memory_space=pltpu.VMEM)
SMEM = pl.BlockSpec(memory_space=pltpu.SMEM)
ANY = pl.BlockSpec(memory_space=pl.ANY)
PARAMS = pltpu.CompilerParams(vmem_limit_bytes=32 * 1024 * 1024)


def swap(value, axis, offset):
    count = lax.axis_size(axis)
    return lax.ppermute(value, axis, [(i, i ^ offset) for i in range(count)])


def start_loads(hbm_ref, vmem_ref, sems):
    size = hbm_ref.shape[0] // CHUNKS
    copies = []
    for chunk in range(CHUNKS):
        part = pl.ds(chunk * size, size)
        copy = pltpu.make_async_copy(hbm_ref.at[part], vmem_ref.at[part], sems.at[chunk])
        copy.start()
        copies.append(copy)
    return copies


def for_each_block(copies, count, body):
    size = count // CHUNKS
    for chunk in range(CHUNKS):
        copies[chunk].wait()

        @pl.loop(chunk * size, (chunk + 1) * size)
        def _(n):
            body(n)


def unit_row(ref, unit):
    row = ref[pl.ds(unit // 2, 1), :]
    return jnp.where(unit % 2 == 0, row[:, :LANES], row[:, LANES:])


def lane_sum(tile):
    return jnp.broadcast_to(jnp.sum(tile, axis=1, keepdims=True), tile.shape)


def pack_pair(first, second):
    lane = lax.broadcasted_iota(jnp.int32, first.shape, 1)
    out = jnp.zeros_like(first)
    for place, rest in ((0, first), (3, second)):
        for part in range(3):
            rounded = rest.astype(BF16).astype(F32)
            out = jnp.where(lane == place + part, rounded, out)
            rest = rest - rounded
    return out.astype(BF16)


def unpack_pair(total):
    lane = lax.broadcasted_iota(jnp.int32, total.shape, 1)
    first = lane_sum(jnp.where(lane < 3, total, 0.0))
    second = lane_sum(jnp.where((lane >= 3) & (lane < 6), total, 0.0))
    return first, second


def next_weight(weight, restart, drift_dual, drift_primal):
    candidate = jnp.sqrt(
        weight * jnp.sqrt((drift_dual + epsilon) / (drift_primal + epsilon))
    )
    return jnp.where(restart == 1, candidate, weight)


def first_max_kernel(rows_ref, cols_ref, a_hbm, row_out, col_out, a, sems, racc, cacc):
    copies = start_loads(a_hbm, a, sems)
    racc[...] = jnp.zeros_like(racc)
    cacc[...] = jnp.zeros_like(cacc)

    def block(n):
        r, c = rows_ref[n], cols_ref[n]
        col = cacc[c]
        for t in range(BLK // 32):
            part = pl.ds(t * 32, 32)
            mag = jnp.abs(a[n, part, :])
            col = jnp.maximum(col, jnp.maximum(mag[:16], mag[16:]))
            racc[r, part, :] = jnp.maximum(
                racc[r, part, :], jnp.maximum(mag[:, :LANES], mag[:, LANES:])
            )
        cacc[c] = col

    for_each_block(copies, a.shape[0], block)
    for b in range(RB):
        flipped = racc[b].astype(F32).T
        row_out[b : b + 1, :] = jnp.max(flipped, axis=0, keepdims=True)
        col_out[b : b + 1, :] = jnp.max(cacc[b].astype(F32), axis=0, keepdims=True)


def max_kernel(
    rows_ref, cols_ref, a_hbm, r_ref, c_ref, row_out, col_out, a, sems, rb, racc, cacc
):
    copies = start_loads(a_hbm, a, sems)
    racc[...] = jnp.zeros_like(racc)
    cacc[...] = jnp.zeros_like(cacc)
    spread_rows(r_ref, rb)

    def block(n):
        r, c = rows_ref[n], cols_ref[n]
        factor = c_ref[pl.ds(c, 1), :]
        col = cacc[c]
        for t in range(BLK // 32):
            part = pl.ds(t * 32, 32)
            mag = jnp.abs(a[n, part, :].astype(F32))
            tall = rb[r, part, :]
            by_row = jnp.concatenate([mag[:, :LANES] * tall, mag[:, LANES:] * tall], 1)
            by_col = mag * factor
            for q in range(4):
                col = jnp.maximum(col, by_row[8 * q : 8 * q + 8])
            racc[r, part, :] = jnp.maximum(
                racc[r, part, :], jnp.maximum(by_col[:, :LANES], by_col[:, LANES:])
            )
        cacc[c] = col

    for_each_block(copies, a.shape[0], block)
    for b in range(RB):
        row_out[b : b + 1, :] = (
            jnp.max(racc[b].T, axis=0, keepdims=True) * r_ref[b : b + 1, :]
        )
        col_out[b : b + 1, :] = (
            jnp.max(cacc[b], axis=0, keepdims=True) * c_ref[b : b + 1, :]
        )


def spread_rows(r_ref, rb):
    for b in range(RB):
        rb[b] = jnp.broadcast_to(r_ref[b : b + 1, :], (LANES, BLK)).T


def row_col_max(rows_of, cols_of, matrix, row_scale, col_scale):
    count = matrix.shape[0]
    first = row_scale is None
    kind = BF16 if first else F32
    scratch = [
        pltpu.VMEM(matrix.shape, BF16),
        pltpu.SemaphoreType.DMA((CHUNKS,)),
    ]
    if not first:
        scratch.append(pltpu.VMEM((RB, BLK, LANES), F32))
    scratch += [
        pltpu.VMEM((RB, BLK, LANES), kind),
        pltpu.VMEM((CB, 16 if first else 8, BLK), kind),
    ]
    operands = (rows_of, cols_of, matrix) + (() if first else (row_scale, col_scale))
    return pl.pallas_call(
        first_max_kernel if first else max_kernel,
        out_shape=(
            jax.ShapeDtypeStruct((RB, BLK), F32),
            jax.ShapeDtypeStruct((CB, BLK), F32),
        ),
        in_specs=[SMEM, SMEM, ANY] + ([] if first else [VMEM, VMEM]),
        out_specs=(VMEM, VMEM),
        scratch_shapes=scratch,
        compiler_params=PARAMS,
        name="first_max" if first else "row_col_max",
    )(*operands)


def exchange_max(row_part, col_part):
    row_step, col_step = 1, 1
    while row_step < lax.axis_size("cols") or col_step < lax.axis_size("rows"):
        row_next = col_next = None
        if row_step < lax.axis_size("cols"):
            row_next = swap(row_part, "cols", row_step)
        if col_step < lax.axis_size("rows"):
            col_next = swap(col_part, "rows", col_step)
        if row_next is not None:
            row_part = jnp.maximum(row_part, row_next)
        if col_next is not None:
            col_part = jnp.maximum(col_part, col_next)
        row_step, col_step = 2 * row_step, 2 * col_step
    return row_part, col_part


def place_pieces(pieces, owners, out):
    for piece, owner in zip(pieces, owners):
        units = piece.shape[1] // LANES
        for k in range(units):
            out[owner * units + k] = piece[:, k * LANES : (k + 1) * LANES]


def fetch_units(ref, first, count):
    return jnp.concatenate([ref[first + k] for k in range(count)], axis=1)


def forward_kernel(scaling, pieces, *refs):
    rows_ref, cols_ref, m_hbm = refs[:3]
    refs = refs[3:]
    if scaling:
        r_ref, c_ref = refs[:2]
        refs = refs[2:]
    piece_refs, refs = refs[:pieces], refs[pieces:]
    if scaling:
        keep, send, m_out, m, sems, x, acc, rb, out_sems = refs
    else:
        keep, send, m, sems, x, acc = refs
    copies = start_loads(m_hbm, m, sems)
    me = lax.axis_index("rows")
    place_pieces(
        [ref[...] for ref in piece_refs], [me ^ o for o in range(pieces)], x
    )
    acc[...] = jnp.zeros_like(acc)
    if scaling:
        spread_rows(r_ref, rb)

    def block(n):
        r, c = rows_ref[n], cols_ref[n]
        if scaling:
            factor = c_ref[pl.ds(c, 1), :]
            for t in range(BLK // 32):
                part = pl.ds(t * 32, 32)
                raw = m[n, part, :].astype(F32)
                tall = rb[r, part, :]
                scaled = jnp.concatenate([raw[:, :LANES] * tall, raw[:, LANES:] * tall], 1)
                m[n, part, :] = (scaled * factor).astype(BF16)
        product = lax.dot_general(
            fetch_units(x, 2 * c, 2),
            m[n],
            (((1,), (1,)), ((), ())),
            preferred_element_type=F32,
        )
        acc[2 * r] += product[:, :LANES]
        acc[2 * r + 1] += product[:, LANES:]

    for_each_block(copies, m.shape[0], block)
    outs = []
    if scaling:
        size = m.shape[0] // CHUNKS
        for chunk in range(CHUNKS):
            part = pl.ds(chunk * size, size)
            copy = pltpu.make_async_copy(m.at[part], m_out.at[part], out_sems.at[chunk])
            copy.start()
            outs.append(copy)
    place = lax.axis_index("cols")
    chip, core = place // 2, place % 2
    units = keep.shape[2] // LANES
    for o in range(keep.shape[0]):
        shard = 2 * (chip ^ o)
        for k in range(units):
            span = pl.ds(k * LANES, LANES)
            keep[o, :, span] = acc[(shard + core) * units + k]
            send[o, :, span] = acc[(shard + 1 - core) * units + k].astype(BF16)
    for copy in outs:
        copy.wait()


def forward(rows_of, cols_of, matrix, pieces, scales=None):
    scenarios = pieces[0].shape[0]
    chips = lax.axis_size("cols") // 2
    width = RB * BLK // lax.axis_size("cols")
    scaling = scales is not None
    out_shape = [
        jax.ShapeDtypeStruct((chips, scenarios, width), F32),
        jax.ShapeDtypeStruct((chips, scenarios, width), BF16),
    ]
    out_specs = [VMEM, VMEM]
    scratch = [
        pltpu.VMEM(matrix.shape, BF16),
        pltpu.SemaphoreType.DMA((CHUNKS,)),
        pltpu.VMEM((CB * BLK // LANES, scenarios, LANES), BF16),
        pltpu.VMEM((RB * BLK // LANES, scenarios, LANES), F32),
    ]
    if scaling:
        out_shape.append(jax.ShapeDtypeStruct(matrix.shape, BF16))
        out_specs.append(ANY)
        scratch += [
            pltpu.VMEM((RB, BLK, LANES), F32),
            pltpu.SemaphoreType.DMA((CHUNKS,)),
        ]
    return pl.pallas_call(
        functools.partial(forward_kernel, scaling, len(pieces)),
        out_shape=out_shape,
        in_specs=[SMEM, SMEM, ANY] + [VMEM] * (len(pieces) + 2 * scaling),
        out_specs=out_specs,
        scratch_shapes=scratch,
        compiler_params=PARAMS,
        name="scale_and_forward" if scaling else "forward",
    )(rows_of, cols_of, matrix, *(scales or ()), *pieces)


def backward_kernel(pieces, *refs):
    rows_ref, cols_ref, m_hbm = refs[:3]
    piece_refs, refs = refs[3 : 3 + pieces], refs[3 + pieces :]
    keep, sends, (m, sems, y, acc) = refs[0], refs[1:-4], refs[-4:]
    copies = start_loads(m_hbm, m, sems)
    place = lax.axis_index("cols")
    chip, core = place // 2, place % 2
    width = RB * BLK // lax.axis_size("cols")
    total = None
    for o, ref in enumerate(piece_refs):
        for half in range(2):
            owner = 2 * (chip ^ o) + (core ^ half)
            place_pieces([ref[half, :, :width]], [owner], y)
            tail = ref[half, :, width:].astype(F32)
            total = tail if total is None else total + tail
    acc[...] = jnp.zeros_like(acc)

    def block(n):
        r, c = rows_ref[n], cols_ref[n]
        product = lax.dot_general(
            fetch_units(y, 2 * r, 2),
            m[n],
            (((1,), (0,)), ((), ())),
            preferred_element_type=F32,
        )
        acc[2 * c] += product[:, :LANES]
        acc[2 * c + 1] += product[:, LANES:]

    for_each_block(copies, m.shape[0], block)
    me = lax.axis_index("rows")
    units = keep.shape[1] // LANES - 1
    tail = pack_pair(*unpack_pair(total))
    for o, out in enumerate((keep,) + tuple(sends)):
        for k in range(units):
            out[:, pl.ds(k * LANES, LANES)] = acc[(me ^ o) * units + k].astype(out.dtype)
        out[:, pl.ds(units * LANES, LANES)] = tail.astype(out.dtype)


def backward(rows_of, cols_of, matrix, pieces):
    scenarios = pieces[0].shape[1]
    width = CB * BLK // lax.axis_size("rows") + LANES
    shape = (scenarios, width)
    others = lax.axis_size("rows") - 1
    return pl.pallas_call(
        functools.partial(backward_kernel, len(pieces)),
        out_shape=[jax.ShapeDtypeStruct(shape, F32)]
        + [jax.ShapeDtypeStruct(shape, BF16)] * others,
        in_specs=[SMEM, SMEM, ANY] + [VMEM] * len(pieces),
        out_specs=[VMEM] * (1 + others),
        scratch_shapes=[
            pltpu.VMEM(matrix.shape, BF16),
            pltpu.SemaphoreType.DMA((CHUNKS,)),
            pltpu.VMEM((RB * BLK // LANES, scenarios, LANES), BF16),
            pltpu.VMEM((CB * BLK // LANES, scenarios, LANES), F32),
        ],
        compiler_params=PARAMS,
        name="backward",
    )(rows_of, cols_of, matrix, *pieces)


def settle(again, stride, totals, new, total, anchor):
    total = total + stride * new
    mean = total / totals
    move = mean - anchor
    return (
        jnp.where(again, mean, new),
        jnp.where(again, 0.0, total),
        jnp.where(again, mean, anchor),
        move * move,
    )


def primal_kernel(first, terms, *refs):
    obj, cap, c_ref, stride_ref, again_ref, weight_ref = refs[:6]
    refs = refs[6:]
    if not first:
        before_ref, wt_ref, state, sums, anchors = refs[:5]
        term_refs = refs[5 : 5 + terms]
        refs = refs[5 + terms :]
    state_out, sums_out, anchors_out, ext, drift, weight_out = refs
    width = obj.shape[1]
    weight = weight_ref[...]
    stride = stride_ref[...]
    again = again_ref[...] == 1
    totals = stride
    if not first:
        totals = wt_ref[...] + stride
        tail = sum(ref[:, width:].astype(F32) for ref in term_refs)
        weight = next_weight(weight, before_ref[...], *unpack_pair(tail))
    weight_out[...] = weight
    step = stride / weight
    place = lax.axis_index("rows")
    units = width // LANES
    moved = jnp.zeros_like(weight)
    for k in range(units):
        span = pl.ds(k * LANES, LANES)
        scale = unit_row(c_ref, place * units + k)
        gradient = obj[:, span] * scale
        upper = cap[:, span] / scale
        if first:
            old = total = anchor = jnp.zeros_like(gradient)
        else:
            old, total, anchor = state[:, span], sums[:, span], anchors[:, span]
            product = sum(ref[:, span].astype(F32) for ref in term_refs)
            gradient = gradient - product
        new = jnp.minimum(jnp.maximum(old - step * gradient, 0.0), upper)
        ext[:, span] = (2.0 * new - old).astype(BF16)
        new, total, anchor, square = settle(again, stride, totals, new, total, anchor)
        state_out[:, span] = new
        sums_out[:, span] = total
        anchors_out[:, span] = anchor
        moved = moved + square
    drift[...] = moved


def primal_update(obj, cap, col_scale, stride, again, weight, rest=None, terms=()):
    shape = obj.shape
    tile = jax.ShapeDtypeStruct((shape[0], LANES), F32)
    whole = jax.ShapeDtypeStruct(shape, F32)
    operands = (obj, cap, col_scale, stride, again, weight) + tuple(rest or ()) + tuple(terms)
    return pl.pallas_call(
        functools.partial(primal_kernel, rest is None, len(terms)),
        out_shape=[whole, whole, whole, jax.ShapeDtypeStruct(shape, BF16), tile, tile],
        in_specs=[VMEM] * len(operands),
        out_specs=[VMEM] * 6,
        compiler_params=PARAMS,
        name="primal_update",
    )(*operands)


def dual_kernel(first, last, terms, *refs):
    demand, r_ref, stride_ref, again_ref, weight_ref, drift_ref = refs[:6]
    refs = refs[6:]
    if not first:
        wt_ref, state, sums, anchors = refs[:4]
        refs = refs[4:]
    term_refs, refs = refs[:terms], refs[terms:]
    state_out, refs = refs[0], refs[1:]
    if last:
        (packed,) = refs
    else:
        sums_out, anchors_out, wt_out, packed = refs
    width = demand.shape[1]
    stride = stride_ref[...]
    again = again_ref[...] == 1
    totals = stride if first else wt_ref[...] + stride
    step = stride * weight_ref[...]
    place = lax.axis_index("cols")
    units = width // LANES
    moved = jnp.zeros_like(step)
    for k in range(units):
        span = pl.ds(k * LANES, LANES)
        scale = unit_row(r_ref, place * units + k)
        image = sum(ref[:, span].astype(F32) for ref in term_refs)
        if first:
            old = total = anchor = jnp.zeros_like(image)
        else:
            old, total, anchor = state[:, span], sums[:, span], anchors[:, span]
        new = old + step * (demand[:, span] * scale - image)
        new, total, anchor, square = settle(again, stride, totals, new, total, anchor)
        state_out[:, span] = new
        if not last:
            sums_out[:, span] = total
            anchors_out[:, span] = anchor
            packed[:, span] = new.astype(BF16)
        moved = moved + square
    dual, primal = lane_sum(moved), lane_sum(drift_ref[...])
    if last:
        lane = lax.broadcasted_iota(jnp.int32, dual.shape, 1)
        packed[...] = jnp.where(lane == 0, dual, jnp.where(lane == 1, primal, 0.0))
    else:
        wt_out[...] = jnp.where(again, 0.0, totals)
        packed[:, width:] = pack_pair(dual, primal)


def dual_update(demand, row_scale, stride, again, weight, drift, rest, terms, last):
    shape = demand.shape
    tile = jax.ShapeDtypeStruct((shape[0], LANES), F32)
    whole = jax.ShapeDtypeStruct(shape, F32)
    operands = (demand, row_scale, stride, again, weight, drift)
    operands += tuple(rest or ()) + tuple(terms)
    if last:
        out_shape = [whole, tile]
    else:
        joined = jax.ShapeDtypeStruct((shape[0], shape[1] + LANES), BF16)
        out_shape = [whole, whole, whole, tile, joined]
    return pl.pallas_call(
        functools.partial(dual_kernel, rest is None, last, len(terms)),
        out_shape=out_shape,
        in_specs=[VMEM] * len(operands),
        out_specs=[VMEM] * len(out_shape),
        compiler_params=PARAMS,
        name="dual_update",
    )(*operands)


def sum_columns(keep, send):
    chips = keep.shape[0]
    near = swap(send, "cols", 1)
    joined = keep + near.astype(F32)
    far = [swap(joined[o].astype(BF16), "cols", 2 * o) for o in range(1, chips)]
    return [joined[0]] + far


def on_device(
    blocks, block_row, block_col, objective, demand, capacity, step_size, restart, primal_weight
):
    matrix = blocks[0, 0]
    rows_of = block_row[0, 0]
    cols_of = block_col[0, 0]
    chips = lax.axis_size("cols") // 2
    row_groups = lax.axis_size("rows")
    scenarios = objective.shape[1]
    obj, cap, need = objective.T, capacity.T, demand.T
    strides = jnp.broadcast_to(step_size[:, :, None], (ITERS, scenarios, LANES))
    agains = jnp.broadcast_to(restart[:, :, None], (ITERS, scenarios, LANES))
    weight = jnp.broadcast_to(primal_weight[:, None], (scenarios, LANES))

    row_scale = col_scale = None
    for _ in range(PASSES):
        row_max, col_max = row_col_max(rows_of, cols_of, matrix, row_scale, col_scale)
        row_max, col_max = exchange_max(row_max, col_max)
        row_scale = (1.0 if row_scale is None else row_scale) / jnp.sqrt(row_max + epsilon)
        col_scale = (1.0 if col_scale is None else col_scale) / jnp.sqrt(col_max + epsilon)

    primal_rest = dual_rest = None
    terms = ()
    for k in range(ITERS):
        state, sums, anchors, ext, drift, weight = primal_update(
            obj, cap, col_scale, strides[k], agains[k], weight, primal_rest, terms
        )
        primal = state
        pieces = [ext] + [swap(ext, "rows", o) for o in range(1, row_groups)]
        if k == 0:
            keep, send, matrix = forward(
                rows_of, cols_of, matrix, pieces, (row_scale, col_scale)
            )
        else:
            keep, send = forward(rows_of, cols_of, matrix, pieces)
        terms = sum_columns(keep, send)
        last = k == ITERS - 1
        outs = dual_update(
            need, row_scale, strides[k], agains[k], weight, drift, dual_rest, terms, last
        )
        if last:
            dual, packed = outs
            break
        dual, dual_sums, dual_anchors, totals, packed = outs
        primal_rest = (agains[k], totals, state, sums, anchors)
        dual_rest = (totals, dual, dual_sums, dual_anchors)
        pair = jnp.stack([packed, swap(packed, "cols", 1)])
        pieces = [pair] + [swap(pair, "cols", 2 * o) for o in range(1, chips)]
        sent = backward(rows_of, cols_of, matrix, pieces)
        terms = [sent[0]] + [swap(sent[o], "rows", o) for o in range(1, row_groups)]

    total = packed + swap(packed, "cols", 1)
    total = total + sum(swap(total, "cols", 2 * o) for o in range(1, chips))
    total = total + sum(swap(total, "rows", o) for o in range(1, row_groups))
    final = next_weight(weight[:, 0], restart[-1], total[:, 0], total[:, 1])
    return (primal.T, dual.T, final)


def solution(mesh):
    in_specs = (
        P("rows", "cols", None, None, None),
        P("rows", "cols", None),
        P("rows", "cols", None),
        P(("cols", "rows"), None),
        P(("rows", "cols"), None),
        P(("cols", "rows"), None),
        P(),
        P(),
        P(),
    )
    out_specs = (P(("cols", "rows"), None), P(("rows", "cols"), None), P())
    return jax.shard_map(
        on_device, mesh=mesh, in_specs=in_specs, out_specs=out_specs, check_vma=False
    )
```

```python
import functools

import jax
import jax.numpy as jnp
from jax import lax
from jax.experimental import pallas as pl
from jax.experimental.pallas import tpu as pltpu
from jax.sharding import PartitionSpec as P

BLK = 256
RB = 16
CB = 16
PASSES = 3
ITERS = 3
LANES = 128

epsilon = 1e-06
F32 = jnp.float32
BF16 = jnp.bfloat16
VMEM = pl.BlockSpec(memory_space=pltpu.VMEM)
SMEM = pl.BlockSpec(memory_space=pltpu.SMEM)
PARAMS = pltpu.CompilerParams(vmem_limit_bytes=32 * 1024 * 1024)


def swap(value, axis, offset):
    count = lax.axis_size(axis)
    return lax.ppermute(value, axis, [(i, i ^ offset) for i in range(count)])


def for_each_block(count, group, body):
    if count == group:
        body(range(count))
    else:

        @pl.loop(0, count // group)
        def _(step):
            body([step * group + k for k in range(group)])


def unit_row(ref, unit):
    row = ref[pl.ds(unit // 2, 1), :]
    return jnp.where(unit % 2 == 0, row[:, :LANES], row[:, LANES:])


def lane_sum(tile):
    return jnp.broadcast_to(jnp.sum(tile, axis=1, keepdims=True), tile.shape)


def split_parts(value):
    parts = []
    for _ in range(3):
        rounded = value.astype(BF16).astype(F32)
        parts.append(rounded)
        value = value - rounded
    return parts


def tail_rows():
    return -(-3 * (lax.axis_size("cols") // 2) // 16) * 16


def to_tail(values, half=0):
    scenarios = values[0][1].shape[0]
    lane = lax.broadcasted_iota(jnp.int32, (scenarios, LANES), 1)
    tile = jnp.zeros((scenarios, LANES), F32)
    for place, value in values:
        for k, part in enumerate(split_parts(value)):
            tile = jnp.where(lane == place + k, part, tile)
    gap = jnp.zeros((LANES // 2 - scenarios, LANES), F32)
    pieces = [jnp.where(half == 0, tile, 0.0), gap, jnp.where(half == 0, 0.0, tile), gap]
    return jnp.concatenate(pieces, axis=0).T[: tail_rows()]


def from_tail(tail, scenarios, first=0, last=LANES):
    rest = jnp.zeros((LANES - tail.shape[0], LANES), F32)
    square = jnp.concatenate([tail, rest], axis=0).T
    tile = square[:scenarios] + square[LANES // 2 : LANES // 2 + scenarios]
    lane = lax.broadcasted_iota(jnp.int32, tile.shape, 1)
    return lane_sum(jnp.where((lane >= first) & (lane < last), tile, 0.0))


def next_weight(weight, restart, drift_dual, drift_primal):
    candidate = jnp.sqrt(
        weight * jnp.sqrt((drift_dual + epsilon) / (drift_primal + epsilon))
    )
    return jnp.where(restart == 1, candidate, weight)


def first_max_kernel(
    places_vmem, a, row_out, col_out, places_ref, sem, racc, cacc
):
    places = pltpu.make_async_copy(places_vmem, places_ref, sem)
    places.start()
    racc[...] = jnp.zeros_like(racc)
    cacc[...] = jnp.zeros_like(cacc)

    def block(n):
        r, c = places_ref[0, n], places_ref[1, n]
        col = cacc[c]
        for t in range(BLK // 32):
            part = pl.ds(t * 32, 32)
            mag = jnp.abs(a[n, part, :])
            col = jnp.maximum(col, jnp.maximum(mag[:16], mag[16:]))
            racc[r, part, :] = jnp.maximum(
                racc[r, part, :], jnp.maximum(mag[:, :LANES], mag[:, LANES:])
            )
        cacc[c] = col

    places.wait()
    for_each_block(a.shape[0], 4, lambda ns: [block(n) for n in ns])
    for b in range(RB):
        flipped = racc[b].astype(F32).T
        row_out[b : b + 1, :] = jnp.max(flipped, axis=0, keepdims=True)
        col_out[b : b + 1, :] = jnp.max(cacc[b].astype(F32), axis=0, keepdims=True)


def max_kernel(
    rows_ref, cols_ref, a, r_ref, c_ref, row_out, col_out, rb, racc, cacc
):
    racc[...] = jnp.zeros_like(racc)
    cacc[...] = jnp.zeros_like(cacc)
    spread_rows(r_ref, rb)

    def block(n):
        r, c = rows_ref[n], cols_ref[n]
        factor = c_ref[pl.ds(c, 1), :]
        col = cacc[c]
        for t in range(BLK // 32):
            part = pl.ds(t * 32, 32)
            mag = jnp.abs(a[n, part, :].astype(F32))
            tall = rb[r, part, :]
            by_row = jnp.concatenate([mag[:, :LANES] * tall, mag[:, LANES:] * tall], 1)
            by_col = mag * factor
            for q in range(4):
                col = jnp.maximum(col, by_row[8 * q : 8 * q + 8])
            racc[r, part, :] = jnp.maximum(
                racc[r, part, :], jnp.maximum(by_col[:, :LANES], by_col[:, LANES:])
            )
        cacc[c] = col

    for_each_block(a.shape[0], 2, lambda ns: [block(n) for n in ns])
    for b in range(RB):
        row_out[b : b + 1, :] = (
            jnp.max(racc[b].T, axis=0, keepdims=True) * r_ref[b : b + 1, :]
        )
        col_out[b : b + 1, :] = (
            jnp.max(cacc[b], axis=0, keepdims=True) * c_ref[b : b + 1, :]
        )


def spread_rows(r_ref, rb):
    for b in range(RB):
        rb[b] = jnp.broadcast_to(r_ref[b : b + 1, :], (LANES, BLK)).T


def first_max(places, matrix):
    count = matrix.shape[0]
    return pl.pallas_call(
        first_max_kernel,
        out_shape=(
            jax.ShapeDtypeStruct((RB, BLK), F32),
            jax.ShapeDtypeStruct((CB, BLK), F32),
        ),
        in_specs=[VMEM, VMEM],
        out_specs=(VMEM, VMEM),
        scratch_shapes=[
            pltpu.SMEM((2, count), jnp.int32),
            pltpu.SemaphoreType.DMA,
            pltpu.VMEM((RB, BLK, LANES), BF16),
            pltpu.VMEM((CB, 16, BLK), BF16),
        ],
        compiler_params=PARAMS,
        name="first_max",
    )(places, matrix)


def row_col_max(rows_of, cols_of, matrix, row_scale, col_scale):
    return pl.pallas_call(
        max_kernel,
        out_shape=(
            jax.ShapeDtypeStruct((RB, BLK), F32),
            jax.ShapeDtypeStruct((CB, BLK), F32),
        ),
        in_specs=[SMEM, SMEM, VMEM, VMEM, VMEM],
        out_specs=(VMEM, VMEM),
        scratch_shapes=[
            pltpu.VMEM((RB, BLK, LANES), F32),
            pltpu.VMEM((RB, BLK, LANES), F32),
            pltpu.VMEM((CB, 8, BLK), F32),
        ],
        compiler_params=PARAMS,
        name="row_col_max",
    )(rows_of, cols_of, matrix, row_scale, col_scale)


def exchange_max(row_part, col_part, last=False):
    row_step, col_step = 1, 1
    while row_step < lax.axis_size("cols") or col_step < lax.axis_size("rows"):
        row_next = col_next = None
        if row_step < lax.axis_size("cols"):
            row_next = swap(row_part, "cols", row_step)
        if col_step < lax.axis_size("rows"):
            col_next = swap(col_part, "rows", col_step)
        if row_next is not None:
            row_part = jnp.maximum(row_part, row_next)
        if col_next is not None:
            col_part = jnp.maximum(col_part, col_next)
        if last and col_step * 2 == lax.axis_size("rows"):
            row_part, col_part = lax.optimization_barrier((row_part, col_part))
        row_step, col_step = 2 * row_step, 2 * col_step
    return row_part, col_part


def fetch_units(ref, first, count):
    return jnp.concatenate([ref[first + k] for k in range(count)], axis=1)


def scale_kernel(rows_ref, cols_ref, a, r_ref, c_ref, m, rb):
    spread_rows(r_ref, rb)

    def block(n):
        r, c = rows_ref[n], cols_ref[n]
        factor = c_ref[pl.ds(c, 1), :]
        for t in range(BLK // 32):
            part = pl.ds(t * 32, 32)
            raw = a[n, part, :].astype(F32)
            tall = rb[r, part, :]
            for half in range(2):
                lanes = slice(half * LANES, (half + 1) * LANES)
                scaled = raw[:, lanes] * tall * factor[:, lanes]
                m[n, part, pl.ds(half * LANES, LANES)] = scaled.astype(BF16)

    for_each_block(m.shape[0], 2, lambda ns: [block(n) for n in ns])


def scale_matrix(rows_of, cols_of, matrix, row_scale, col_scale):
    return pl.pallas_call(
        scale_kernel,
        out_shape=jax.ShapeDtypeStruct(matrix.shape, BF16),
        in_specs=[SMEM, SMEM, VMEM, VMEM, VMEM],
        out_specs=VMEM,
        scratch_shapes=[pltpu.VMEM((RB, BLK, LANES), F32)],
        compiler_params=PARAMS,
        name="scale_matrix",
    )(rows_of, cols_of, matrix, row_scale, col_scale)


def product_scratch(scenarios):
    return [
        pltpu.VMEM((CB * BLK // LANES, scenarios, LANES), BF16),
        pltpu.VMEM((RB * BLK // LANES, scenarios, LANES), F32),
    ]


def block_products(ns, sources, targets, x, m, acc, dims):
    products = [
        lax.dot_general(
            fetch_units(x, 2 * sources[n], 2), m[n], dims, preferred_element_type=F32
        )
        for n in ns
    ]
    for n, product in zip(ns, products):
        unit = 2 * targets[n]
        acc[unit] += product[:, :LANES]
        acc[unit + 1] += product[:, LANES:]


def forward_kernel(pieces, *refs):
    rows_ref, cols_ref, m, drift = refs[:4]
    piece_refs = refs[4 : 4 + pieces]
    keep, send, x, acc = refs[4 + pieces :]
    scenarios = x.shape[1]
    me = lax.axis_index("rows")
    units = x.shape[0] // pieces
    for o, piece in enumerate(piece_refs):
        for k in range(units):
            x[(me ^ o) * units + k] = piece[k * scenarios : (k + 1) * scenarios, :]
    acc[...] = jnp.zeros_like(acc)
    count = m.shape[0]
    dims = (((1,), (1,)), ((), ()))
    for_each_block(
        count, count, lambda ns: block_products(ns, cols_ref, rows_ref, x, m, acc, dims)
    )
    me, core = lax.axis_index("cols") // 2, lax.axis_index("cols") % 2
    shards = lax.axis_size("cols")
    units = acc.shape[0] // shards
    for chip in range(shards // 2):
        for k in range(units):
            rows = pl.ds((chip * units + k) * scenarios, scenarios)
            keep[rows, :] = acc[(2 * chip + core) * units + k]
            send[rows, :] = acc[(2 * chip + 1 - core) * units + k].astype(BF16)
    tail = to_tail([(3 * me, lane_sum(drift[...]))], core)
    rows = pl.ds(keep.shape[0] - tail_rows(), tail_rows())
    keep[rows, :] = tail
    send[rows, :] = tail.astype(BF16)


def half_rows(scenarios):
    return RB * BLK // 2 // LANES * scenarios + tail_rows()


def forward(rows_of, cols_of, matrix, drift, pieces):
    scenarios = drift.shape[0]
    rows = half_rows(scenarios)
    return pl.pallas_call(
        functools.partial(forward_kernel, len(pieces)),
        out_shape=[
            jax.ShapeDtypeStruct((rows, LANES), F32),
            jax.ShapeDtypeStruct((rows, LANES), BF16),
        ],
        in_specs=[SMEM, SMEM, VMEM, VMEM] + [VMEM] * len(pieces),
        out_specs=[VMEM] * 2,
        scratch_shapes=product_scratch(scenarios),
        compiler_params=PARAMS,
        name="forward",
    )(rows_of, cols_of, matrix, drift, *pieces)


def backward_kernel(*refs):
    rows_ref, cols_ref, m, own, other, drift, keep = refs[:7]
    sends, (y, acc) = refs[7:-2], refs[-2:]
    scenarios = y.shape[1]
    core = lax.axis_index("cols") % 2
    shards = lax.axis_size("cols")
    units = y.shape[0] // shards
    for half, ref in ((core, own), (1 - core, other)):
        for chip in range(shards // 2):
            for k in range(units):
                start = (chip * units + k) * scenarios
                y[(2 * chip + half) * units + k] = ref[start : start + scenarios, :]
    acc[...] = jnp.zeros_like(acc)
    count = m.shape[0]
    dims = (((1,), (0,)), ((), ()))
    for_each_block(
        count, count, lambda ns: block_products(ns, rows_ref, cols_ref, y, m, acc, dims)
    )
    tail = own[own.shape[0] - tail_rows() :, :].astype(F32)
    tail = tail + other[other.shape[0] - tail_rows() :, :].astype(F32)
    tail = to_tail([(0, from_tail(tail, scenarios)), (3, drift[...])])
    me = lax.axis_index("rows")
    units = acc.shape[0] // (1 + len(sends))
    for o, out in enumerate((keep,) + tuple(sends)):
        for k in range(units):
            out[pl.ds(k * scenarios, scenarios), :] = acc[(me ^ o) * units + k].astype(
                out.dtype
            )
        out[pl.ds(units * scenarios, tail_rows()), :] = tail.astype(out.dtype)


def backward(rows_of, cols_of, matrix, own, other, drift):
    scenarios = drift.shape[0]
    groups = lax.axis_size("rows")
    shape = (CB * BLK // groups // LANES * scenarios + tail_rows(), LANES)
    return pl.pallas_call(
        backward_kernel,
        out_shape=[jax.ShapeDtypeStruct(shape, F32)]
        + [jax.ShapeDtypeStruct(shape, BF16)] * (groups - 1),
        in_specs=[SMEM, SMEM, VMEM, VMEM, VMEM, VMEM],
        out_specs=[VMEM] * groups,
        scratch_shapes=product_scratch(scenarios),
        compiler_params=PARAMS,
        name="backward",
    )(rows_of, cols_of, matrix, own, other, drift)


def settle(again, stride, totals, new, total, anchor):
    total = total + stride * new
    mean = total / totals
    move = mean - anchor
    return (
        jnp.where(again, mean, new),
        jnp.where(again, 0.0, total),
        jnp.where(again, mean, anchor),
        move * move,
    )


def primal_kernel(first, last, terms, *refs):
    obj, cap, c_ref, stride_ref, again_ref, weight_ref = refs[:6]
    refs = refs[6:]
    if not first:
        before_ref, wt_ref, state, sums, anchors = refs[:5]
        term_refs = refs[5 : 5 + terms]
        refs = refs[5 + terms :]
    state_out, ext, drift, weight_out = refs[:4]
    width = obj.shape[1]
    weight = weight_ref[...]
    stride = stride_ref[...]
    again = again_ref[...] == 1
    totals = stride
    if not first:
        totals = wt_ref[...] + stride
        scenarios = weight.shape[0]
        tail = sum(ref[ref.shape[0] - tail_rows() :, :].astype(F32) for ref in term_refs)
        drift_dual = from_tail(tail, scenarios, 0, 3)
        drift_primal = from_tail(tail, scenarios, 3, 6)
        weight = next_weight(weight, before_ref[...], drift_dual, drift_primal)
    weight_out[...] = weight
    step = stride / weight
    place = lax.axis_index("rows")
    units = width // LANES
    moved = jnp.zeros_like(weight)
    for k in range(units):
        span = pl.ds(k * LANES, LANES)
        scale = unit_row(c_ref, place * units + k)
        gradient = obj[:, span] * scale
        upper = cap[:, span] / scale
        if first:
            old = total = anchor = jnp.zeros_like(gradient)
        else:
            old, total, anchor = state[:, span], sums[:, span], anchors[:, span]
            rows = pl.ds(k * obj.shape[0], obj.shape[0])
            product = sum(ref[rows, :].astype(F32) for ref in term_refs)
            gradient = gradient - product
        new = jnp.minimum(jnp.maximum(old - step * gradient, 0.0), upper)
        ext[pl.ds(k * obj.shape[0], obj.shape[0]), :] = (2.0 * new - old).astype(BF16)
        new, total, anchor, square = settle(again, stride, totals, new, total, anchor)
        state_out[:, span] = new
        if not last:
            sums_out, anchors_out = refs[4:]
            sums_out[:, span] = total
            anchors_out[:, span] = anchor
        moved = moved + square
    drift[...] = moved


def primal_update(obj, cap, col_scale, stride, again, weight, rest, terms, last):
    shape = obj.shape
    tile = jax.ShapeDtypeStruct((shape[0], LANES), F32)
    whole = jax.ShapeDtypeStruct(shape, F32)
    ext = jax.ShapeDtypeStruct((shape[1] // LANES * shape[0], LANES), BF16)
    operands = (obj, cap, col_scale, stride, again, weight) + tuple(rest or ()) + tuple(terms)
    return pl.pallas_call(
        functools.partial(primal_kernel, rest is None, last, len(terms)),
        out_shape=[whole, ext, tile, tile] + [whole] * (0 if last else 2),
        in_specs=[VMEM] * len(operands),
        out_specs=[VMEM] * (4 if last else 6),
        compiler_params=PARAMS,
        name="primal_update",
    )(*operands)


def dual_kernel(first, last, chips, *refs):
    stride_ref, again_ref, weight_ref = refs[:3]
    refs = refs[3:]
    if first:
        r_ref, refs = refs[0], refs[1:]
        demands, refs = refs[:chips], refs[chips:]
    else:
        need, wt_ref, state, sums, anchors = refs[:5]
        refs = refs[5:]
    parts, refs = (refs[:2], refs[2:4]), refs[4:]
    if last:
        out, drifts, state_out = refs
    else:
        if first:
            need, refs = refs[0], refs[1:]
        state_out, sums_out, anchors_out, wt_out, packed, drift_out = refs
    stride = stride_ref[...]
    scenarios = stride.shape[0]
    again = again_ref[...] == 1
    totals = stride if first else wt_ref[...] + stride
    step = stride * weight_ref[...]
    place = lax.axis_index("cols")
    me, core = place // 2, place % 2
    count = state_out.shape[0] // scenarios
    units = count // chips
    if first:
        for o, demand in enumerate(demands):
            for k in range(units):
                scale = unit_row(r_ref, (2 * (me ^ o) + core) * units + k)
                start = pl.multiple_of(((me ^ o) * units + k) * scenarios, 8)
                need[pl.ds(start, scenarios), :] = (
                    demand[:, k * LANES : (k + 1) * LANES] * scale
                )
    moved = jnp.zeros_like(step)
    for k in range(count):
        span = pl.ds(k * scenarios, scenarios)
        part, place = divmod(k, count // 2)
        rows = pl.ds(place * scenarios, scenarios)
        image = sum(ref[rows, :].astype(F32) for ref in parts[part])
        if first:
            old = total = anchor = jnp.zeros_like(image)
        else:
            old, total, anchor = state[span, :], sums[span, :], anchors[span, :]
        new = old + step * (need[span, :] - image)
        new, total, anchor, square = settle(again, stride, totals, new, total, anchor)
        state_out[span, :] = new
        if not last:
            sums_out[span, :] = total
            anchors_out[span, :] = anchor
            packed[span, :] = new.astype(BF16)
        moved = moved + square
    start = count // 2 * scenarios
    tail = sum(ref[start:, :].astype(F32) for ref in parts[1])
    dual, primal = lane_sum(moved), from_tail(tail, scenarios)
    if last:
        lane = lax.broadcasted_iota(jnp.int32, dual.shape, 1)
        drifts[...] = jnp.where(lane == 0, dual, jnp.where(lane == 1, primal, 0.0))
        for k in range(units):
            start = pl.multiple_of((me * units + k) * scenarios, 8)
            out[:, k * LANES : (k + 1) * LANES] = state_out[pl.ds(start, scenarios), :]
    else:
        wt_out[...] = jnp.where(again, 0.0, totals)
        packed[pl.ds(count * scenarios, tail_rows()), :] = to_tail([(0, dual)], core).astype(BF16)
        drift_out[...] = primal


def dual_update(stride, again, weight, rest, terms, width, row_scale=None, last=False):
    first = row_scale is not None
    chips = lax.axis_size("cols") // 2
    scenarios = stride.shape[0]
    rows = half_rows(scenarios)
    tile = jax.ShapeDtypeStruct((scenarios, LANES), F32)
    half = jax.ShapeDtypeStruct((rows - tail_rows(), LANES), F32)
    operands = (stride, again, weight) + ((row_scale,) if first else ())
    operands += tuple(rest) + tuple(terms)
    scratch = []
    if last:
        out_shape = [jax.ShapeDtypeStruct((scenarios, width), F32), tile]
        scratch = [pltpu.VMEM(half.shape, F32)]
    else:
        packed = jax.ShapeDtypeStruct((rows, LANES), BF16)
        out_shape = [half] * (3 + first) + [tile, packed, tile]
    return pl.pallas_call(
        functools.partial(dual_kernel, first, last, chips),
        out_shape=out_shape,
        in_specs=[VMEM] * len(operands),
        out_specs=[VMEM] * len(out_shape),
        scratch_shapes=scratch,
        compiler_params=PARAMS,
        name="dual_update",
    )(*operands)


def sum_columns(keep, send):
    chips = lax.axis_size("cols") // 2
    joined = keep + swap(send, "cols", 1).astype(F32)
    middle = (joined.shape[0] - tail_rows()) // 2
    parts = [joined[:middle], joined[middle:]]
    steps = [1 << k for k in range(chips.bit_length() - 1)]
    for k in range(len(steps)):
        got = [
            swap(part.astype(BF16), "cols", 2 * order[k])
            for part, order in zip(parts, (steps, steps[::-1]))
        ]
        if k == len(steps) - 1:
            return [parts[0], got[0], parts[1], got[1]]
        parts = [part + more.astype(F32) for part, more in zip(parts, got)]


def on_device(
    blocks, block_row, block_col, objective, demand, capacity, step_size, restart, primal_weight
):
    rows_of = block_row[0, 0]
    cols_of = block_col[0, 0]
    chips = lax.axis_size("cols") // 2
    row_groups = lax.axis_size("rows")
    scenarios = objective.shape[1]
    obj, cap, need = objective.T, capacity.T, demand.T
    strides = jnp.broadcast_to(step_size[:, :, None], (ITERS, scenarios, LANES))
    agains = jnp.broadcast_to(restart[:, :, None], (ITERS, scenarios, LANES))
    weight = jnp.broadcast_to(primal_weight[:, None], (scenarios, LANES))

    matrix = blocks[0, 0]
    row_top, col_top = first_max(jnp.stack([rows_of, cols_of]), matrix)
    row_top, col_top = exchange_max(row_top, col_top)
    row_scale = 1.0 / jnp.sqrt(row_top + epsilon)
    col_scale = 1.0 / jnp.sqrt(col_top + epsilon)
    for sweep in range(1, PASSES):
        row_top, col_top = row_col_max(rows_of, cols_of, matrix, row_scale, col_scale)
        row_top, col_top = exchange_max(row_top, col_top, sweep == PASSES - 1)
        row_scale = row_scale / jnp.sqrt(row_top + epsilon)
        col_scale = col_scale / jnp.sqrt(col_top + epsilon)

    primal_rest = dual_rest = None
    terms = ()
    for k in range(ITERS):
        last = k == ITERS - 1
        primal, ext, drift, weight, *more = primal_update(
            obj, cap, col_scale, strides[k], agains[k], weight, primal_rest, terms, last
        )
        if k == 0:
            row_scale, need = lax.optimization_barrier((row_scale, need))
        pieces = [ext] + [swap(ext, "rows", o) for o in range(1, row_groups)]
        if k == 0:
            matrix = scale_matrix(rows_of, cols_of, matrix, row_scale, col_scale)
            dual_rest = [need] + [swap(need, "cols", 2 * o) for o in range(1, chips)]
            pieces, dual_rest = lax.optimization_barrier((pieces, dual_rest))
        keep, send = forward(rows_of, cols_of, matrix, drift, pieces)
        terms = sum_columns(keep, send)
        outs = dual_update(
            strides[k],
            agains[k],
            weight,
            dual_rest,
            terms,
            need.shape[1],
            row_scale=row_scale if k == 0 else None,
            last=last,
        )
        if last:
            dual, packed = outs
            break
        if k == 0:
            demands, outs = outs[0], outs[1:]
        dual, dual_sums, dual_anchors, totals, packed, drift = outs
        primal_rest = (agains[k], totals, primal, *more)
        dual_rest = (demands, totals, dual, dual_sums, dual_anchors)
        sent = backward(rows_of, cols_of, matrix, packed, swap(packed, "cols", 1), drift)
        terms = [sent[0]] + [swap(sent[o], "rows", o) for o in range(1, row_groups)]

    other = swap(packed, "cols", 1)
    lane = lax.broadcasted_iota(jnp.int32, packed.shape, 1)
    total = packed + jnp.where(lane == 0, other, 0.0)
    step = 1
    while step < row_groups:
        total = total + swap(total, "rows", step)
        step *= 2
    final = next_weight(weight[:, 0], restart[-1], total[:, 0], total[:, 1])
    return (primal.T, dual.T, final)


def solution(mesh):
    in_specs = (
        P("rows", "cols", None, None, None),
        P("rows", "cols", None),
        P("rows", "cols", None),
        P(("cols", "rows"), None),
        P(("rows", "cols"), None),
        P(("cols", "rows"), None),
        P(),
        P(),
        P(),
    )
    out_specs = (P(("cols", "rows"), None), P(("rows", "cols"), None), P())
    return jax.shard_map(
        on_device, mesh=mesh, in_specs=in_specs, out_specs=out_specs, check_vma=False
    )
```

```python
import functools

import jax
import jax.numpy as jnp
from jax import lax
from jax.experimental import pallas as pl
from jax.experimental.pallas import tpu as pltpu
from jax.sharding import PartitionSpec as P

BLK = 256
RB = 16
CB = 16
PASSES = 3
ITERS = 3
LANES = 128

epsilon = 1e-06
F32 = jnp.float32
BF16 = jnp.bfloat16
VMEM = pl.BlockSpec(memory_space=pltpu.VMEM)
SMEM = pl.BlockSpec(memory_space=pltpu.SMEM)
PARAMS = pltpu.CompilerParams(vmem_limit_bytes=32 * 1024 * 1024)


def offsets(groups):
    return [0] + [o ^ 3 if o < 3 else o for o in range(1, groups)]


def swap(value, axis, offset):
    if offset == 0:
        return value
    count = lax.axis_size(axis)
    return lax.ppermute(value, axis, [(i, i ^ offset) for i in range(count)])


def for_each_block(count, group, body):
    if count == group:
        body(range(count))
    else:

        @pl.loop(0, count // group)
        def _(step):
            body([step * group + k for k in range(group)])


def unit_row(ref, unit):
    row = ref[pl.ds(unit // 2, 1), :]
    return jnp.where(unit % 2 == 0, row[:, :LANES], row[:, LANES:])


def lane_sum(tile):
    return jnp.broadcast_to(jnp.sum(tile, axis=1, keepdims=True), tile.shape)


def split_parts(value):
    parts = []
    for _ in range(3):
        rounded = value.astype(BF16).astype(F32)
        parts.append(rounded)
        value = value - rounded
    return parts


def tail_rows():
    return -(-3 * (lax.axis_size("cols") // 2) // 16) * 16


def to_tail(values, half=0):
    scenarios = values[0][1].shape[0]
    lane = lax.broadcasted_iota(jnp.int32, (scenarios, LANES), 1)
    tile = jnp.zeros((scenarios, LANES), F32)
    for place, value in values:
        for k, part in enumerate(split_parts(value)):
            tile = jnp.where(lane == place + k, part, tile)
    gap = jnp.zeros((LANES // 2 - scenarios, LANES), F32)
    pieces = [jnp.where(half == 0, tile, 0.0), gap, jnp.where(half == 0, 0.0, tile), gap]
    return jnp.concatenate(pieces, axis=0).T[: tail_rows()]


def to_rows(values):
    scenarios = values[0].shape[0]
    lane = lax.broadcasted_iota(jnp.int32, values[0].shape, 1)
    tile = jnp.zeros(values[0].shape, F32)
    for place, value in enumerate(values):
        tile = jnp.where(lane == place, value, tile)
    rest = jnp.zeros((LANES - scenarios, LANES), F32)
    return jnp.concatenate([tile, rest], axis=0).T[:8]


def from_tail(tail, scenarios, first=0, last=LANES):
    rest = jnp.zeros((LANES - tail.shape[0], LANES), F32)
    square = jnp.concatenate([tail, rest], axis=0).T
    tile = square[:scenarios] + square[LANES // 2 : LANES // 2 + scenarios]
    lane = lax.broadcasted_iota(jnp.int32, tile.shape, 1)
    return lane_sum(jnp.where((lane >= first) & (lane < last), tile, 0.0))


def next_weight(weight, restart, drift_dual, drift_primal):
    candidate = jnp.sqrt(
        weight * jnp.sqrt((drift_dual + epsilon) / (drift_primal + epsilon))
    )
    return jnp.where(restart == 1, candidate, weight)


def first_max_kernel(
    places_vmem, a, row_out, col_out, same, places_ref, sem, racc, cacc
):
    del same
    places = pltpu.make_async_copy(places_vmem, places_ref, sem)
    places.start()
    racc[...] = jnp.zeros_like(racc)
    cacc[...] = jnp.zeros_like(cacc)

    def block(n):
        r, c = places_ref[0, n], places_ref[1, n]
        col = cacc[c]
        for t in range(BLK // 32):
            part = pl.ds(t * 32, 32)
            mag = jnp.abs(a[n, part, :])
            col = jnp.maximum(col, jnp.maximum(mag[:16], mag[16:]))
            racc[r, part, :] = jnp.maximum(
                racc[r, part, :], jnp.maximum(mag[:, :LANES], mag[:, LANES:])
            )
        cacc[c] = col

    places.wait()
    for_each_block(a.shape[0], 4, lambda ns: [block(n) for n in ns])
    for b in range(RB):
        flipped = racc[b].astype(F32).T
        row_out[b : b + 1, :] = jnp.max(flipped, axis=0, keepdims=True)
        col_out[b : b + 1, :] = jnp.max(cacc[b].astype(F32), axis=0, keepdims=True)


def max_kernel(
    rows_ref, cols_ref, a, r_ref, c_ref, row_out, col_out, rb, racc, cacc
):
    racc[...] = jnp.zeros_like(racc)
    cacc[...] = jnp.zeros_like(cacc)
    spread_rows(r_ref, rb)

    def block(n):
        r, c = rows_ref[n], cols_ref[n]
        factor = c_ref[pl.ds(c, 1), :]
        col = cacc[c]
        for t in range(BLK // 32):
            part = pl.ds(t * 32, 32)
            mag = jnp.abs(a[n, part, :].astype(F32))
            tall = rb[r, part, :]
            by_row = jnp.concatenate([mag[:, :LANES] * tall, mag[:, LANES:] * tall], 1)
            by_col = mag * factor
            for q in range(4):
                col = jnp.maximum(col, by_row[8 * q : 8 * q + 8])
            racc[r, part, :] = jnp.maximum(
                racc[r, part, :], jnp.maximum(by_col[:, :LANES], by_col[:, LANES:])
            )
        cacc[c] = col

    for_each_block(a.shape[0], 2, lambda ns: [block(n) for n in ns])
    for b in range(RB):
        row_out[b : b + 1, :] = (
            jnp.max(racc[b].T, axis=0, keepdims=True) * r_ref[b : b + 1, :]
        )
        col_out[b : b + 1, :] = (
            jnp.max(cacc[b], axis=0, keepdims=True) * c_ref[b : b + 1, :]
        )


def spread_rows(r_ref, rb):
    for b in range(RB):
        rb[b] = jnp.broadcast_to(r_ref[b : b + 1, :], (LANES, BLK)).T


def first_max(places, matrix):
    count = matrix.shape[0]
    return pl.pallas_call(
        first_max_kernel,
        out_shape=(
            jax.ShapeDtypeStruct((RB, BLK), F32),
            jax.ShapeDtypeStruct((CB, BLK), F32),
            jax.ShapeDtypeStruct(matrix.shape, BF16),
        ),
        in_specs=[VMEM, VMEM],
        out_specs=(VMEM, VMEM, VMEM),
        input_output_aliases={1: 2},
        scratch_shapes=[
            pltpu.SMEM((2, count), jnp.int32),
            pltpu.SemaphoreType.DMA,
            pltpu.VMEM((RB, BLK, LANES), BF16),
            pltpu.VMEM((CB, 16, BLK), BF16),
        ],
        compiler_params=PARAMS,
        name="first_max",
    )(places, matrix)


def row_col_max(rows_of, cols_of, matrix, row_scale, col_scale):
    return pl.pallas_call(
        max_kernel,
        out_shape=(
            jax.ShapeDtypeStruct((RB, BLK), F32),
            jax.ShapeDtypeStruct((CB, BLK), F32),
        ),
        in_specs=[SMEM, SMEM, VMEM, VMEM, VMEM],
        out_specs=(VMEM, VMEM),
        scratch_shapes=[
            pltpu.VMEM((RB, BLK, LANES), F32),
            pltpu.VMEM((RB, BLK, LANES), F32),
            pltpu.VMEM((CB, 8, BLK), F32),
        ],
        compiler_params=PARAMS,
        name="row_col_max",
    )(rows_of, cols_of, matrix, row_scale, col_scale)


def exchange_max(row_part, col_part, last=False):
    row_step, col_step = 1, 1
    while row_step < lax.axis_size("cols") or col_step < lax.axis_size("rows"):
        row_next = col_next = None
        if row_step < lax.axis_size("cols"):
            row_next = swap(row_part, "cols", row_step)
        if col_step < lax.axis_size("rows"):
            col_next = swap(col_part, "rows", col_step)
        if row_next is not None:
            row_part = jnp.maximum(row_part, row_next)
        if col_next is not None:
            col_part = jnp.maximum(col_part, col_next)
        if last and col_step * 2 == lax.axis_size("rows"):
            row_part, col_part = lax.optimization_barrier((row_part, col_part))
        row_step, col_step = 2 * row_step, 2 * col_step
    return row_part, col_part


def fetch_units(ref, first, count):
    return jnp.concatenate([ref[first + k] for k in range(count)], axis=1)


def scale_kernel(rows_ref, cols_ref, a, r_ref, c_ref, m, rb):
    spread_rows(r_ref, rb)

    def block(n):
        r, c = rows_ref[n], cols_ref[n]
        factor = c_ref[pl.ds(c, 1), :]
        for t in range(BLK // 32):
            part = pl.ds(t * 32, 32)
            raw = a[n, part, :].astype(F32)
            tall = rb[r, part, :]
            for half in range(2):
                lanes = slice(half * LANES, (half + 1) * LANES)
                scaled = raw[:, lanes] * tall * factor[:, lanes]
                m[n, part, pl.ds(half * LANES, LANES)] = scaled.astype(BF16)

    for_each_block(m.shape[0], 2, lambda ns: [block(n) for n in ns])


def scale_matrix(rows_of, cols_of, matrix, row_scale, col_scale):
    return pl.pallas_call(
        scale_kernel,
        out_shape=jax.ShapeDtypeStruct(matrix.shape, BF16),
        in_specs=[SMEM, SMEM, VMEM, VMEM, VMEM],
        out_specs=VMEM,
        scratch_shapes=[pltpu.VMEM((RB, BLK, LANES), F32)],
        compiler_params=PARAMS,
        name="scale_matrix",
    )(rows_of, cols_of, matrix, row_scale, col_scale)


def product_scratch(scenarios):
    return [
        pltpu.VMEM((CB * BLK // LANES, scenarios, LANES), BF16),
        pltpu.VMEM((RB * BLK // LANES, scenarios, LANES), F32),
    ]


def block_products(ns, sources, targets, x, m, acc, dims):
    products = [
        lax.dot_general(
            fetch_units(x, 2 * sources[n], 2), m[n], dims, preferred_element_type=F32
        )
        for n in ns
    ]
    for n, product in zip(ns, products):
        unit = 2 * targets[n]
        acc[unit] += product[:, :LANES]
        acc[unit + 1] += product[:, LANES:]


def forward_kernel(pieces, *refs):
    rows_ref, cols_ref, m, drift = refs[:4]
    piece_refs = refs[4 : 4 + pieces]
    keep, send, x, acc = refs[4 + pieces :]
    scenarios = x.shape[1]
    me = lax.axis_index("rows")
    units = x.shape[0] // pieces
    for o, piece in zip(offsets(pieces), piece_refs):
        for k in range(units):
            x[(me ^ o) * units + k] = piece[k * scenarios : (k + 1) * scenarios, :]
    acc[...] = jnp.zeros_like(acc)
    count = m.shape[0]
    dims = (((1,), (1,)), ((), ()))
    for_each_block(
        count, count, lambda ns: block_products(ns, cols_ref, rows_ref, x, m, acc, dims)
    )
    me, core = lax.axis_index("cols") // 2, lax.axis_index("cols") % 2
    shards = lax.axis_size("cols")
    units = acc.shape[0] // shards
    for chip in range(shards // 2):
        for k in range(units):
            rows = pl.ds((chip * units + k) * scenarios, scenarios)
            keep[rows, :] = acc[(2 * chip + core) * units + k]
            send[rows, :] = acc[(2 * chip + 1 - core) * units + k].astype(BF16)
    tail = to_tail([(3 * me, lane_sum(drift[...]))], core)
    rows = pl.ds(keep.shape[0] - tail_rows(), tail_rows())
    keep[rows, :] = tail
    send[rows, :] = tail.astype(BF16)


def half_rows(scenarios):
    return RB * BLK // 2 // LANES * scenarios + tail_rows()


def forward(rows_of, cols_of, matrix, drift, pieces):
    scenarios = drift.shape[0]
    rows = half_rows(scenarios)
    return pl.pallas_call(
        functools.partial(forward_kernel, len(pieces)),
        out_shape=[
            jax.ShapeDtypeStruct((rows, LANES), F32),
            jax.ShapeDtypeStruct((rows, LANES), BF16),
        ],
        in_specs=[SMEM, SMEM, VMEM, VMEM] + [VMEM] * len(pieces),
        out_specs=[VMEM] * 2,
        scratch_shapes=product_scratch(scenarios),
        compiler_params=PARAMS,
        name="forward",
    )(rows_of, cols_of, matrix, drift, *pieces)


def backward_kernel(*refs):
    rows_ref, cols_ref, m, own, other, drift, keep = refs[:7]
    sends, (y, acc) = refs[7:-2], refs[-2:]
    scenarios = y.shape[1]
    core = lax.axis_index("cols") % 2
    shards = lax.axis_size("cols")
    units = y.shape[0] // shards
    for half, ref in ((core, own), (1 - core, other)):
        for chip in range(shards // 2):
            for k in range(units):
                start = (chip * units + k) * scenarios
                y[(2 * chip + half) * units + k] = ref[start : start + scenarios, :]
    acc[...] = jnp.zeros_like(acc)
    count = m.shape[0]
    dims = (((1,), (0,)), ((), ()))
    for_each_block(
        count, count, lambda ns: block_products(ns, rows_ref, cols_ref, y, m, acc, dims)
    )
    tail = own[own.shape[0] - tail_rows() :, :].astype(F32)
    tail = tail + other[other.shape[0] - tail_rows() :, :].astype(F32)
    tail = to_tail([(0, from_tail(tail, scenarios)), (3, drift[...])])
    me = lax.axis_index("rows")
    units = acc.shape[0] // (1 + len(sends))
    for o, out in zip(offsets(1 + len(sends)), (keep,) + tuple(sends)):
        for k in range(units):
            out[pl.ds(k * scenarios, scenarios), :] = acc[(me ^ o) * units + k].astype(
                out.dtype
            )
        out[pl.ds(units * scenarios, tail_rows()), :] = tail.astype(out.dtype)


def backward(rows_of, cols_of, matrix, own, other, drift):
    scenarios = drift.shape[0]
    groups = lax.axis_size("rows")
    shape = (CB * BLK // groups // LANES * scenarios + tail_rows(), LANES)
    return pl.pallas_call(
        backward_kernel,
        out_shape=[jax.ShapeDtypeStruct(shape, F32)]
        + [jax.ShapeDtypeStruct(shape, BF16)] * (groups - 1),
        in_specs=[SMEM, SMEM, VMEM, VMEM, VMEM, VMEM],
        out_specs=[VMEM] * groups,
        scratch_shapes=product_scratch(scenarios),
        compiler_params=PARAMS,
        name="backward",
    )(rows_of, cols_of, matrix, own, other, drift)


def settle(again, stride, totals, new, total, anchor):
    total = total + stride * new
    mean = total / totals
    move = mean - anchor
    return (
        jnp.where(again, mean, new),
        jnp.where(again, 0.0, total),
        jnp.where(again, mean, anchor),
        move * move,
    )


def column(ref, lane):
    return jnp.broadcast_to(ref[:, lane : lane + 1], (ref.shape[0], LANES))


def primal_kernel(k, terms, *refs):
    first, last = k == 0, k == ITERS - 1
    obj, cap, c_ref, plan = refs[:4]
    refs = refs[4:]
    if not first:
        weight_ref, wt_ref, state, sums, anchors = refs[:5]
        term_refs = refs[5 : 5 + terms]
        refs = refs[5 + terms :]
    state_out, ext, drift, weight_out = refs[:4]
    width = obj.shape[1]
    stride = column(plan, k)
    again = column(plan, ITERS + k) == 1
    if first:
        totals, weight = stride, column(plan, 2 * ITERS)
    else:
        totals, weight = wt_ref[...] + stride, weight_ref[...]
        scenarios = weight.shape[0]
        tail = sum(ref[ref.shape[0] - tail_rows() :, :].astype(F32) for ref in term_refs)
        drift_dual = from_tail(tail, scenarios, 0, 3)
        drift_primal = from_tail(tail, scenarios, 3, 6)
        weight = next_weight(weight, column(plan, ITERS + k - 1), drift_dual, drift_primal)
    weight_out[...] = weight
    step = stride / weight
    place = lax.axis_index("rows")
    units = width // LANES
    moved = jnp.zeros_like(weight)
    for u in range(units):
        span = pl.ds(u * LANES, LANES)
        scale = unit_row(c_ref, place * units + u)
        gradient = obj[:, span] * scale
        upper = cap[:, span] / scale
        if first:
            old = total = anchor = jnp.zeros_like(gradient)
        else:
            old, total, anchor = state[:, span], sums[:, span], anchors[:, span]
            rows = pl.ds(u * obj.shape[0], obj.shape[0])
            product = sum(ref[rows, :].astype(F32) for ref in term_refs)
            gradient = gradient - product
        new = jnp.minimum(jnp.maximum(old - step * gradient, 0.0), upper)
        ext[pl.ds(u * obj.shape[0], obj.shape[0]), :] = (2.0 * new - old).astype(BF16)
        new, total, anchor, square = settle(again, stride, totals, new, total, anchor)
        state_out[:, span] = new
        if not last:
            sums_out, anchors_out = refs[4:]
            sums_out[:, span] = total
            anchors_out[:, span] = anchor
        moved = moved + square
    drift[...] = moved


def primal_update(k, obj, cap, col_scale, plan, rest, terms):
    shape = obj.shape
    tile = jax.ShapeDtypeStruct((shape[0], LANES), F32)
    whole = jax.ShapeDtypeStruct(shape, F32)
    ext = jax.ShapeDtypeStruct((shape[1] // LANES * shape[0], LANES), BF16)
    operands = (obj, cap, col_scale, plan) + tuple(rest) + tuple(terms)
    last = k == ITERS - 1
    return pl.pallas_call(
        functools.partial(primal_kernel, k, len(terms)),
        out_shape=[whole, ext, tile, tile] + [whole] * (0 if last else 2),
        in_specs=[VMEM] * len(operands),
        out_specs=[VMEM] * (4 if last else 6),
        compiler_params=PARAMS,
        name="primal_update",
    )(*operands)


def dual_kernel(iteration, chips, *refs):
    first, last = iteration == 0, iteration == ITERS - 1
    plan, weight_ref = refs[:2]
    refs = refs[2:]
    if first:
        r_ref, refs = refs[0], refs[1:]
        demands, refs = refs[:chips], refs[chips:]
    else:
        need, wt_ref, state, sums, anchors = refs[:5]
        refs = refs[5:]
    parts, refs = (refs[:2], refs[2:4]), refs[4:]
    if last:
        out, drifts, weights, state_out = refs
    else:
        if first:
            need, refs = refs[0], refs[1:]
        state_out, sums_out, anchors_out, wt_out, packed, drift_out = refs
    stride = column(plan, iteration)
    scenarios = stride.shape[0]
    again = column(plan, ITERS + iteration) == 1
    totals = stride if first else wt_ref[...] + stride
    step = stride * weight_ref[...]
    place = lax.axis_index("cols")
    me, core = place // 2, place % 2
    count = state_out.shape[0] // scenarios
    units = count // chips
    if first:
        for o, demand in enumerate(demands):
            for k in range(units):
                scale = unit_row(r_ref, (2 * (me ^ o) + core) * units + k)
                start = pl.multiple_of(((me ^ o) * units + k) * scenarios, 8)
                need[pl.ds(start, scenarios), :] = (
                    demand[:, k * LANES : (k + 1) * LANES] * scale
                )
    moved = jnp.zeros_like(step)
    for k in range(count):
        span = pl.ds(k * scenarios, scenarios)
        part, place = divmod(k, count // 2)
        rows = pl.ds(place * scenarios, scenarios)
        image = sum(ref[rows, :].astype(F32) for ref in parts[part])
        if first:
            old = total = anchor = jnp.zeros_like(image)
        else:
            old, total, anchor = state[span, :], sums[span, :], anchors[span, :]
        new = old + step * (need[span, :] - image)
        new, total, anchor, square = settle(again, stride, totals, new, total, anchor)
        state_out[span, :] = new
        if not last:
            sums_out[span, :] = total
            anchors_out[span, :] = anchor
            packed[span, :] = new.astype(BF16)
        moved = moved + square
    start = count // 2 * scenarios
    tail = sum(ref[start:, :].astype(F32) for ref in parts[1])
    dual, primal = lane_sum(moved), from_tail(tail, scenarios)
    if last:
        drifts[...] = to_rows([dual, primal])
        weights[...] = to_rows([weight_ref[...]])
        for k in range(units):
            start = pl.multiple_of((me * units + k) * scenarios, 8)
            out[:, k * LANES : (k + 1) * LANES] = state_out[pl.ds(start, scenarios), :]
    else:
        wt_out[...] = jnp.where(again, 0.0, totals)
        packed[pl.ds(count * scenarios, tail_rows()), :] = to_tail([(0, dual)], core).astype(BF16)
        drift_out[...] = primal


def dual_update(iteration, plan, weight, rest, terms, width):
    first, last = iteration == 0, iteration == ITERS - 1
    chips = lax.axis_size("cols") // 2
    scenarios = plan.shape[0]
    rows = half_rows(scenarios)
    tile = jax.ShapeDtypeStruct((scenarios, LANES), F32)
    half = jax.ShapeDtypeStruct((rows - tail_rows(), LANES), F32)
    operands = (plan, weight) + tuple(rest) + tuple(terms)
    scratch = []
    if last:
        rows = jax.ShapeDtypeStruct((8, LANES), F32)
        out_shape = [jax.ShapeDtypeStruct((scenarios, width), F32), rows, rows]
        scratch = [pltpu.VMEM(half.shape, F32)]
    else:
        packed = jax.ShapeDtypeStruct((rows, LANES), BF16)
        out_shape = [half] * (3 + first) + [tile, packed, tile]
    return pl.pallas_call(
        functools.partial(dual_kernel, iteration, chips),
        out_shape=out_shape,
        in_specs=[VMEM] * len(operands),
        out_specs=[VMEM] * len(out_shape),
        scratch_shapes=scratch,
        compiler_params=PARAMS,
        name="dual_update",
    )(*operands)


def copy_kernel(source, out):
    out[...] = source[...]


def hand_over(value):
    return pl.pallas_call(
        copy_kernel,
        out_shape=jax.ShapeDtypeStruct(value.shape, value.dtype),
        in_specs=[VMEM],
        out_specs=VMEM,
        compiler_params=PARAMS,
        name="hand_over",
    )(value)


def sum_columns(keep, send):
    chips = lax.axis_size("cols") // 2
    joined = keep + swap(send, "cols", 1).astype(F32)
    middle = (joined.shape[0] - tail_rows()) // 2
    parts = [joined[:middle], joined[middle:]]
    steps = [1 << k for k in range(chips.bit_length() - 1)]
    for k in range(len(steps)):
        got = [
            swap(part.astype(BF16), "cols", 2 * order[k])
            for part, order in zip(parts, (steps, steps[::-1]))
        ]
        if k == len(steps) - 1:
            return [parts[0], got[0], parts[1], got[1]]
        parts = [part + more.astype(F32) for part, more in zip(parts, got)]


def on_device(
    blocks, block_row, block_col, objective, demand, capacity, step_size, restart, primal_weight
):
    rows_of = block_row[0, 0]
    cols_of = block_col[0, 0]
    chips = lax.axis_size("cols") // 2
    row_groups = lax.axis_size("rows")
    scenarios = objective.shape[1]
    obj, cap, need = objective.T, capacity.T, demand.T
    plan = jnp.concatenate([step_size, restart.astype(F32), primal_weight[None]]).T
    plan = jnp.pad(plan, ((0, 0), (0, LANES - plan.shape[1])))

    matrix = blocks[0, 0]
    row_top, col_top, matrix = first_max(jnp.stack([rows_of, cols_of]), matrix)
    row_top, col_top = exchange_max(row_top, col_top)
    row_scale = 1.0 / jnp.sqrt(row_top + epsilon)
    col_scale = 1.0 / jnp.sqrt(col_top + epsilon)
    for sweep in range(1, PASSES):
        row_top, col_top = row_col_max(rows_of, cols_of, matrix, row_scale, col_scale)
        if sweep == PASSES - 1:
            row_top, need = lax.optimization_barrier((row_top, need))
        row_top, col_top = exchange_max(row_top, col_top, sweep == PASSES - 1)
        row_scale = row_scale / jnp.sqrt(row_top + epsilon)
        col_scale = col_scale / jnp.sqrt(col_top + epsilon)

    primal_rest = terms = ()
    for k in range(ITERS):
        last = k == ITERS - 1
        primal, ext, drift, weight, *more = primal_update(
            k, obj, cap, col_scale, plan, primal_rest, terms
        )
        pieces = [swap(ext, "rows", o) for o in offsets(row_groups)]
        if k == 0:
            matrix = scale_matrix(rows_of, cols_of, matrix, row_scale, col_scale)
            dual_rest = [need] + [swap(need, "cols", 2 * o) for o in range(1, chips)]
            pieces, dual_rest = lax.optimization_barrier((pieces, dual_rest))
            dual_rest = [row_scale] + dual_rest
        keep, send = forward(rows_of, cols_of, matrix, drift, pieces)
        terms = sum_columns(keep, send)
        outs = dual_update(k, plan, weight, dual_rest, terms, need.shape[1])
        if last:
            dual, packed, weight = outs
            break
        if k == 0:
            demands, outs = outs[0], outs[1:]
        dual, dual_sums, dual_anchors, totals, packed, drift = outs
        primal_rest = (weight, totals, primal, *more)
        dual_rest = (demands, totals, dual, dual_sums, dual_anchors)
        sent = backward(rows_of, cols_of, matrix, packed, swap(packed, "cols", 1), drift)
        terms = [swap(value, "rows", o) for value, o in zip(sent, offsets(row_groups))]

    other = swap(packed, "cols", 1)
    row = lax.broadcasted_iota(jnp.int32, packed.shape, 0)
    total = packed + jnp.where(row == 0, other, 0.0)
    step = 1
    while step < row_groups:
        total = total + swap(total, "rows", step)
        step *= 2
    weight, drift_dual, drift_primal = (
        value[:scenarios] for value in (weight[0], total[0], total[1])
    )
    final = next_weight(weight, restart[-1], drift_dual, drift_primal)
    return (hand_over(primal).T, hand_over(dual).T, final)


def solution(mesh):
    in_specs = (
        P("rows", "cols", None, None, None),
        P("rows", "cols", None),
        P("rows", "cols", None),
        P(("cols", "rows"), None),
        P(("rows", "cols"), None),
        P(("cols", "rows"), None),
        P(),
        P(),
        P(),
    )
    out_specs = (P(("cols", "rows"), None), P(("rows", "cols"), None), P())
    return jax.shard_map(
        on_device, mesh=mesh, in_specs=in_specs, out_specs=out_specs, check_vma=False
    )
```

```python
import functools

import jax
import jax.numpy as jnp
from jax import lax
from jax.experimental import pallas as pl
from jax.experimental.pallas import tpu as pltpu
from jax.sharding import PartitionSpec as P

BLK = 256
RB = 16
CB = 16
PASSES = 3
ITERS = 3
LANES = 128

epsilon = 1e-06
F32 = jnp.float32
BF16 = jnp.bfloat16
VMEM = pl.BlockSpec(memory_space=pltpu.VMEM)
SMEM = pl.BlockSpec(memory_space=pltpu.SMEM)
PARAMS = pltpu.CompilerParams(vmem_limit_bytes=32 * 1024 * 1024)


def offsets(groups):
    return [0] + [o ^ 3 if o < 3 else o for o in range(1, groups)]


def swap(value, axis, offset):
    if offset == 0:
        return value
    count = lax.axis_size(axis)
    return lax.ppermute(value, axis, [(i, i ^ offset) for i in range(count)])


def for_each_block(count, group, body):
    if count == group:
        body(range(count))
    else:

        @pl.loop(0, count // group)
        def _(step):
            body([step * group + k for k in range(group)])


def unit_row(ref, unit):
    row = ref[pl.ds(unit // 2, 1), :]
    return jnp.where(unit % 2 == 0, row[:, :LANES], row[:, LANES:])


def lane_sum(tile):
    return jnp.broadcast_to(jnp.sum(tile, axis=1, keepdims=True), tile.shape)


def split_parts(value):
    parts = []
    for _ in range(3):
        rounded = value.astype(BF16).astype(F32)
        parts.append(rounded)
        value = value - rounded
    return parts


def tail_rows():
    return -(-3 * (lax.axis_size("cols") // 2) // 16) * 16


def to_tail(values, half=0):
    scenarios = values[0][1].shape[0]
    lane = lax.broadcasted_iota(jnp.int32, (scenarios, LANES), 1)
    tile = jnp.zeros((scenarios, LANES), F32)
    for place, value in values:
        for k, part in enumerate(split_parts(value)):
            tile = jnp.where(lane == place + k, part, tile)
    gap = jnp.zeros((LANES // 2 - scenarios, LANES), F32)
    pieces = [jnp.where(half == 0, tile, 0.0), gap, jnp.where(half == 0, 0.0, tile), gap]
    return jnp.concatenate(pieces, axis=0).T[: tail_rows()]


def to_rows(values):
    scenarios = values[0].shape[0]
    lane = lax.broadcasted_iota(jnp.int32, values[0].shape, 1)
    tile = jnp.zeros(values[0].shape, F32)
    for place, value in enumerate(values):
        tile = jnp.where(lane == place, value, tile)
    rest = jnp.zeros((LANES - scenarios, LANES), F32)
    return jnp.concatenate([tile, rest], axis=0).T[:8]


def from_tail(tail, scenarios, first=0, last=LANES):
    rest = jnp.zeros((LANES - tail.shape[0], LANES), F32)
    square = jnp.concatenate([tail, rest], axis=0).T
    tile = square[:scenarios] + square[LANES // 2 : LANES // 2 + scenarios]
    lane = lax.broadcasted_iota(jnp.int32, tile.shape, 1)
    return lane_sum(jnp.where((lane >= first) & (lane < last), tile, 0.0))


def next_weight(weight, restart, drift_dual, drift_primal):
    candidate = jnp.sqrt(
        weight * jnp.sqrt((drift_dual + epsilon) / (drift_primal + epsilon))
    )
    return jnp.where(restart == 1, candidate, weight)


def first_max_kernel(
    places_vmem, a, row_out, col_out, same, places_ref, sem, racc, cacc
):
    del same
    places = pltpu.make_async_copy(places_vmem, places_ref, sem)
    places.start()
    racc[...] = jnp.zeros_like(racc)
    cacc[...] = jnp.zeros_like(cacc)

    def block(n):
        r, c = places_ref[0, n], places_ref[1, n]
        col = cacc[c]
        for t in range(BLK // 32):
            part = pl.ds(t * 32, 32)
            mag = jnp.abs(a[n, part, :])
            col = jnp.maximum(col, jnp.maximum(mag[:16], mag[16:]))
            racc[r, part, :] = jnp.maximum(
                racc[r, part, :], jnp.maximum(mag[:, :LANES], mag[:, LANES:])
            )
        cacc[c] = col

    places.wait()
    for_each_block(a.shape[0], 4, lambda ns: [block(n) for n in ns])
    for b in range(RB):
        flipped = racc[b].astype(F32).T
        row_out[b : b + 1, :] = jnp.max(flipped, axis=0, keepdims=True)
        col_out[b : b + 1, :] = jnp.max(cacc[b].astype(F32), axis=0, keepdims=True)


def max_kernel(
    rows_ref, cols_ref, a, r_ref, c_ref, row_out, col_out, rb, racc, cacc
):
    racc[...] = jnp.zeros_like(racc)
    cacc[...] = jnp.zeros_like(cacc)
    spread_rows(r_ref, rb)

    def block(n):
        r, c = rows_ref[n], cols_ref[n]
        factor = c_ref[pl.ds(c, 1), :]
        col = cacc[c]
        for t in range(BLK // 32):
            part = pl.ds(t * 32, 32)
            mag = jnp.abs(a[n, part, :].astype(F32))
            tall = rb[r, part, :]
            by_row = jnp.concatenate([mag[:, :LANES] * tall, mag[:, LANES:] * tall], 1)
            by_col = mag * factor
            for q in range(4):
                col = jnp.maximum(col, by_row[8 * q : 8 * q + 8])
            racc[r, part, :] = jnp.maximum(
                racc[r, part, :], jnp.maximum(by_col[:, :LANES], by_col[:, LANES:])
            )
        cacc[c] = col

    for_each_block(a.shape[0], 2, lambda ns: [block(n) for n in ns])
    for b in range(RB):
        row_out[b : b + 1, :] = (
            jnp.max(racc[b].T, axis=0, keepdims=True) * r_ref[b : b + 1, :]
        )
        col_out[b : b + 1, :] = (
            jnp.max(cacc[b], axis=0, keepdims=True) * c_ref[b : b + 1, :]
        )


def spread_rows(r_ref, rb):
    for b in range(RB):
        rb[b] = jnp.broadcast_to(r_ref[b : b + 1, :], (LANES, BLK)).T


def first_max(places, matrix):
    count = matrix.shape[0]
    return pl.pallas_call(
        first_max_kernel,
        out_shape=(
            jax.ShapeDtypeStruct((RB, BLK), F32),
            jax.ShapeDtypeStruct((CB, BLK), F32),
            jax.ShapeDtypeStruct(matrix.shape, BF16),
        ),
        in_specs=[VMEM, VMEM],
        out_specs=(VMEM, VMEM, VMEM),
        input_output_aliases={1: 2},
        scratch_shapes=[
            pltpu.SMEM((2, count), jnp.int32),
            pltpu.SemaphoreType.DMA,
            pltpu.VMEM((RB, BLK, LANES), BF16),
            pltpu.VMEM((CB, 16, BLK), BF16),
        ],
        compiler_params=PARAMS,
        name="first_max",
    )(places, matrix)


def row_col_max(rows_of, cols_of, matrix, row_scale, col_scale):
    return pl.pallas_call(
        max_kernel,
        out_shape=(
            jax.ShapeDtypeStruct((RB, BLK), F32),
            jax.ShapeDtypeStruct((CB, BLK), F32),
        ),
        in_specs=[SMEM, SMEM, VMEM, VMEM, VMEM],
        out_specs=(VMEM, VMEM),
        scratch_shapes=[
            pltpu.VMEM((RB, BLK, LANES), F32),
            pltpu.VMEM((RB, BLK, LANES), F32),
            pltpu.VMEM((CB, 8, BLK), F32),
        ],
        compiler_params=PARAMS,
        name="row_col_max",
    )(rows_of, cols_of, matrix, row_scale, col_scale)


def exchange_max(row_part, col_part):
    row_step, col_step = 1, 1
    while col_step < lax.axis_size("rows"):
        row_next = swap(row_part, "cols", row_step)
        col_next = swap(col_part, "rows", col_step)
        row_part = jnp.maximum(row_part, row_next)
        col_part = jnp.maximum(col_part, col_next)
        row_step, col_step = 2 * row_step, 2 * col_step

    def rest(part):
        step = row_step
        while step < lax.axis_size("cols"):
            part = jnp.maximum(part, swap(part, "cols", step))
            step *= 2
        return part

    return row_part, col_part, rest


def fetch_units(ref, first, count):
    return jnp.concatenate([ref[first + k] for k in range(count)], axis=1)


def scale_kernel(rows_ref, cols_ref, a, r_ref, c_ref, m, rb):
    spread_rows(r_ref, rb)

    def block(n):
        r, c = rows_ref[n], cols_ref[n]
        factor = c_ref[pl.ds(c, 1), :]
        for t in range(BLK // 32):
            part = pl.ds(t * 32, 32)
            raw = a[n, part, :].astype(F32)
            tall = rb[r, part, :]
            for half in range(2):
                lanes = slice(half * LANES, (half + 1) * LANES)
                scaled = raw[:, lanes] * tall * factor[:, lanes]
                m[n, part, pl.ds(half * LANES, LANES)] = scaled.astype(BF16)

    for_each_block(m.shape[0], 2, lambda ns: [block(n) for n in ns])


def scale_matrix(rows_of, cols_of, matrix, row_scale, col_scale):
    return pl.pallas_call(
        scale_kernel,
        out_shape=jax.ShapeDtypeStruct(matrix.shape, BF16),
        in_specs=[SMEM, SMEM, VMEM, VMEM, VMEM],
        out_specs=VMEM,
        scratch_shapes=[pltpu.VMEM((RB, BLK, LANES), F32)],
        compiler_params=PARAMS,
        name="scale_matrix",
    )(rows_of, cols_of, matrix, row_scale, col_scale)


def product_scratch(scenarios):
    return [
        pltpu.VMEM((CB * BLK // LANES, scenarios, LANES), BF16),
        pltpu.VMEM((RB * BLK // LANES, scenarios, LANES), F32),
    ]


def block_products(ns, sources, targets, x, m, acc, dims):
    products = [
        lax.dot_general(
            fetch_units(x, 2 * sources[n], 2), m[n], dims, preferred_element_type=F32
        )
        for n in ns
    ]
    for n, product in zip(ns, products):
        unit = 2 * targets[n]
        acc[unit] += product[:, :LANES]
        acc[unit + 1] += product[:, LANES:]


def forward_kernel(pieces, *refs):
    rows_ref, cols_ref, m, drift = refs[:4]
    piece_refs = refs[4 : 4 + pieces]
    keep, send, x, acc = refs[4 + pieces :]
    scenarios = x.shape[1]
    me = lax.axis_index("rows")
    units = x.shape[0] // pieces
    for o, piece in zip(offsets(pieces), piece_refs):
        for k in range(units):
            x[(me ^ o) * units + k] = piece[k * scenarios : (k + 1) * scenarios, :]
    acc[...] = jnp.zeros_like(acc)
    count = m.shape[0]
    dims = (((1,), (1,)), ((), ()))
    for_each_block(
        count, count, lambda ns: block_products(ns, cols_ref, rows_ref, x, m, acc, dims)
    )
    me, core = lax.axis_index("cols") // 2, lax.axis_index("cols") % 2
    shards = lax.axis_size("cols")
    units = acc.shape[0] // shards
    for chip in range(shards // 2):
        for k in range(units):
            rows = pl.ds((chip * units + k) * scenarios, scenarios)
            keep[rows, :] = acc[(2 * chip + core) * units + k]
            send[rows, :] = acc[(2 * chip + 1 - core) * units + k].astype(BF16)
    tail = to_tail([(3 * me, lane_sum(drift[...]))], core)
    rows = pl.ds(keep.shape[0] - tail_rows(), tail_rows())
    keep[rows, :] = tail
    send[rows, :] = tail.astype(BF16)


def half_rows(scenarios):
    return RB * BLK // 2 // LANES * scenarios + tail_rows()


def forward(rows_of, cols_of, matrix, drift, pieces):
    scenarios = drift.shape[0]
    rows = half_rows(scenarios)
    return pl.pallas_call(
        functools.partial(forward_kernel, len(pieces)),
        out_shape=[
            jax.ShapeDtypeStruct((rows, LANES), F32),
            jax.ShapeDtypeStruct((rows, LANES), BF16),
        ],
        in_specs=[SMEM, SMEM, VMEM, VMEM] + [VMEM] * len(pieces),
        out_specs=[VMEM] * 2,
        scratch_shapes=product_scratch(scenarios),
        compiler_params=PARAMS,
        name="forward",
    )(rows_of, cols_of, matrix, drift, *pieces)


def backward_kernel(*refs):
    rows_ref, cols_ref, m, own, other, drift, keep = refs[:7]
    sends, (y, acc) = refs[7:-2], refs[-2:]
    scenarios = y.shape[1]
    core = lax.axis_index("cols") % 2
    shards = lax.axis_size("cols")
    units = y.shape[0] // shards
    for half, ref in ((core, own), (1 - core, other)):
        for chip in range(shards // 2):
            for k in range(units):
                start = (chip * units + k) * scenarios
                y[(2 * chip + half) * units + k] = ref[start : start + scenarios, :]
    acc[...] = jnp.zeros_like(acc)
    count = m.shape[0]
    dims = (((1,), (0,)), ((), ()))
    for_each_block(
        count, count, lambda ns: block_products(ns, rows_ref, cols_ref, y, m, acc, dims)
    )
    tail = own[own.shape[0] - tail_rows() :, :].astype(F32)
    tail = tail + other[other.shape[0] - tail_rows() :, :].astype(F32)
    tail = to_tail([(0, from_tail(tail, scenarios)), (3, drift[...])])
    me = lax.axis_index("rows")
    units = acc.shape[0] // (1 + len(sends))
    for o, out in zip(offsets(1 + len(sends)), (keep,) + tuple(sends)):
        for k in range(units):
            out[pl.ds(k * scenarios, scenarios), :] = acc[(me ^ o) * units + k].astype(
                out.dtype
            )
        out[pl.ds(units * scenarios, tail_rows()), :] = tail.astype(out.dtype)


def backward(rows_of, cols_of, matrix, own, other, drift):
    scenarios = drift.shape[0]
    groups = lax.axis_size("rows")
    shape = (CB * BLK // groups // LANES * scenarios + tail_rows(), LANES)
    return pl.pallas_call(
        backward_kernel,
        out_shape=[jax.ShapeDtypeStruct(shape, F32)]
        + [jax.ShapeDtypeStruct(shape, BF16)] * (groups - 1),
        in_specs=[SMEM, SMEM, VMEM, VMEM, VMEM, VMEM],
        out_specs=[VMEM] * groups,
        scratch_shapes=product_scratch(scenarios),
        compiler_params=PARAMS,
        name="backward",
    )(rows_of, cols_of, matrix, own, other, drift)


def settle(again, stride, totals, new, total, anchor):
    total = total + stride * new
    mean = total / totals
    move = mean - anchor
    return (
        jnp.where(again, mean, new),
        jnp.where(again, 0.0, total),
        jnp.where(again, mean, anchor),
        move * move,
    )


def plan_kernel(steps, restarts, weight, out, square):
    square[...] = jnp.zeros_like(square)
    count, scenarios = steps.shape
    square[:count, :scenarios] = steps[...]
    square[count : 2 * count, :scenarios] = restarts[...].astype(F32)
    square[2 * count : 2 * count + 1, :scenarios] = weight[...]
    out[...] = square[...].T[:scenarios]


def make_plan(steps, restarts, weight):
    return pl.pallas_call(
        plan_kernel,
        out_shape=jax.ShapeDtypeStruct((steps.shape[1], LANES), F32),
        in_specs=[VMEM] * 3,
        out_specs=VMEM,
        scratch_shapes=[pltpu.VMEM((LANES, LANES), F32)],
        compiler_params=PARAMS,
        name="make_plan",
    )(steps, restarts, weight)


def column(ref, lane):
    return jnp.broadcast_to(ref[:, lane : lane + 1], (ref.shape[0], LANES))


def primal_kernel(k, terms, *refs):
    first, last = k == 0, k == ITERS - 1
    obj, cap, c_ref, plan = refs[:4]
    refs = refs[4:]
    if not first:
        weight_ref, wt_ref, state, sums, anchors = refs[:5]
        term_refs = refs[5 : 5 + terms]
        refs = refs[5 + terms :]
    state_out, ext, drift, weight_out = refs[:4]
    width = obj.shape[1]
    stride = column(plan, k)
    again = column(plan, ITERS + k) == 1
    if first:
        totals, weight = stride, column(plan, 2 * ITERS)
    else:
        totals, weight = wt_ref[...] + stride, weight_ref[...]
        scenarios = weight.shape[0]
        tail = sum(ref[ref.shape[0] - tail_rows() :, :].astype(F32) for ref in term_refs)
        drift_dual = from_tail(tail, scenarios, 0, 3)
        drift_primal = from_tail(tail, scenarios, 3, 6)
        weight = next_weight(weight, column(plan, ITERS + k - 1), drift_dual, drift_primal)
    weight_out[...] = weight
    step = stride / weight
    place = lax.axis_index("rows")
    units = width // LANES
    moved = jnp.zeros_like(weight)
    for u in range(units):
        span = pl.ds(u * LANES, LANES)
        scale = unit_row(c_ref, place * units + u)
        gradient = obj[:, span] * scale
        upper = cap[:, span] / scale
        if first:
            old = total = anchor = jnp.zeros_like(gradient)
        else:
            old, total, anchor = state[:, span], sums[:, span], anchors[:, span]
            rows = pl.ds(u * obj.shape[0], obj.shape[0])
            product = sum(ref[rows, :].astype(F32) for ref in term_refs)
            gradient = gradient - product
        new = jnp.minimum(jnp.maximum(old - step * gradient, 0.0), upper)
        ext[pl.ds(u * obj.shape[0], obj.shape[0]), :] = (2.0 * new - old).astype(BF16)
        new, total, anchor, square = settle(again, stride, totals, new, total, anchor)
        state_out[:, span] = new
        if not last:
            sums_out, anchors_out = refs[4:]
            sums_out[:, span] = total
            anchors_out[:, span] = anchor
        moved = moved + square
    drift[...] = moved


def primal_update(k, obj, cap, col_scale, plan, rest, terms):
    shape = obj.shape
    tile = jax.ShapeDtypeStruct((shape[0], LANES), F32)
    whole = jax.ShapeDtypeStruct(shape, F32)
    ext = jax.ShapeDtypeStruct((shape[1] // LANES * shape[0], LANES), BF16)
    operands = (obj, cap, col_scale, plan) + tuple(rest) + tuple(terms)
    last = k == ITERS - 1
    return pl.pallas_call(
        functools.partial(primal_kernel, k, len(terms)),
        out_shape=[whole, ext, tile, tile] + [whole] * (0 if last else 2),
        in_specs=[VMEM] * len(operands),
        out_specs=[VMEM] * (4 if last else 6),
        compiler_params=PARAMS,
        name="primal_update",
    )(*operands)


def dual_kernel(iteration, chips, *refs):
    first, last = iteration == 0, iteration == ITERS - 1
    plan, weight_ref = refs[:2]
    refs = refs[2:]
    if first:
        r_ref, refs = refs[0], refs[1:]
        demands, refs = refs[:chips], refs[chips:]
    else:
        need, wt_ref, state, sums, anchors = refs[:5]
        refs = refs[5:]
    parts, refs = (refs[:2], refs[2:4]), refs[4:]
    if last:
        out, drifts, weights, state_out = refs
    else:
        if first:
            need, refs = refs[0], refs[1:]
        state_out, sums_out, anchors_out, wt_out, packed, drift_out = refs
    stride = column(plan, iteration)
    scenarios = stride.shape[0]
    again = column(plan, ITERS + iteration) == 1
    totals = stride if first else wt_ref[...] + stride
    step = stride * weight_ref[...]
    place = lax.axis_index("cols")
    me, core = place // 2, place % 2
    count = state_out.shape[0] // scenarios
    units = count // chips
    if first:
        for o, demand in enumerate(demands):
            for k in range(units):
                scale = unit_row(r_ref, (2 * (me ^ o) + core) * units + k)
                start = pl.multiple_of(((me ^ o) * units + k) * scenarios, 8)
                need[pl.ds(start, scenarios), :] = (
                    demand[:, k * LANES : (k + 1) * LANES] * scale
                )
    moved = jnp.zeros_like(step)
    for k in range(count):
        span = pl.ds(k * scenarios, scenarios)
        part, place = divmod(k, count // 2)
        rows = pl.ds(place * scenarios, scenarios)
        image = sum(ref[rows, :].astype(F32) for ref in parts[part])
        if first:
            old = total = anchor = jnp.zeros_like(image)
        else:
            old, total, anchor = state[span, :], sums[span, :], anchors[span, :]
        new = old + step * (need[span, :] - image)
        new, total, anchor, square = settle(again, stride, totals, new, total, anchor)
        state_out[span, :] = new
        if not last:
            sums_out[span, :] = total
            anchors_out[span, :] = anchor
            packed[span, :] = new.astype(BF16)
        moved = moved + square
    start = count // 2 * scenarios
    tail = sum(ref[start:, :].astype(F32) for ref in parts[1])
    dual, primal = lane_sum(moved), from_tail(tail, scenarios)
    if last:
        drifts[...] = to_rows([dual, primal])
        weights[...] = to_rows([weight_ref[...]])
        for k in range(units):
            start = pl.multiple_of((me * units + k) * scenarios, 8)
            out[:, k * LANES : (k + 1) * LANES] = state_out[pl.ds(start, scenarios), :]
    else:
        wt_out[...] = jnp.where(again, 0.0, totals)
        packed[pl.ds(count * scenarios, tail_rows()), :] = to_tail([(0, dual)], core).astype(BF16)
        drift_out[...] = primal


def dual_update(iteration, plan, weight, rest, terms, width):
    first, last = iteration == 0, iteration == ITERS - 1
    chips = lax.axis_size("cols") // 2
    scenarios = plan.shape[0]
    rows = half_rows(scenarios)
    tile = jax.ShapeDtypeStruct((scenarios, LANES), F32)
    half = jax.ShapeDtypeStruct((rows - tail_rows(), LANES), F32)
    operands = (plan, weight) + tuple(rest) + tuple(terms)
    scratch = []
    if last:
        rows = jax.ShapeDtypeStruct((8, LANES), F32)
        out_shape = [jax.ShapeDtypeStruct((scenarios, width), F32), rows, rows]
        scratch = [pltpu.VMEM(half.shape, F32)]
    else:
        packed = jax.ShapeDtypeStruct((rows, LANES), BF16)
        out_shape = [half] * (3 + first) + [tile, packed, tile]
    return pl.pallas_call(
        functools.partial(dual_kernel, iteration, chips),
        out_shape=out_shape,
        in_specs=[VMEM] * len(operands),
        out_specs=[VMEM] * len(out_shape),
        scratch_shapes=scratch,
        compiler_params=PARAMS,
        name="dual_update",
    )(*operands)


def copy_kernel(source, out):
    out[...] = source[...]


def hand_over(value):
    return pl.pallas_call(
        copy_kernel,
        out_shape=jax.ShapeDtypeStruct(value.shape, value.dtype),
        in_specs=[VMEM],
        out_specs=VMEM,
        compiler_params=PARAMS,
        name="hand_over",
    )(value)


def sum_columns(keep, send):
    chips = lax.axis_size("cols") // 2
    joined = keep + swap(send, "cols", 1).astype(F32)
    middle = (joined.shape[0] - tail_rows()) // 2
    parts = [joined[:middle], joined[middle:]]
    steps = [1 << k for k in range(chips.bit_length() - 1)]
    for k in range(len(steps)):
        got = [
            swap(part.astype(BF16), "cols", 2 * order[k])
            for part, order in zip(parts, (steps, steps[::-1]))
        ]
        if k == len(steps) - 1:
            return [parts[0], got[0], parts[1], got[1]]
        parts = [part + more.astype(F32) for part, more in zip(parts, got)]


def on_device(
    blocks, block_row, block_col, objective, demand, capacity, step_size, restart, primal_weight
):
    rows_of = block_row[0, 0]
    cols_of = block_col[0, 0]
    chips = lax.axis_size("cols") // 2
    row_groups = lax.axis_size("rows")
    scenarios = objective.shape[1]
    obj, cap, need = objective.T, capacity.T, demand.T
    plan = make_plan(step_size, restart, primal_weight[None])

    matrix = blocks[0, 0]
    row_top, col_top, matrix = first_max(jnp.stack([rows_of, cols_of]), matrix)
    row_part, col_top, rest = exchange_max(row_top, col_top)
    row_scale = 1.0 / jnp.sqrt(rest(row_part) + epsilon)
    col_scale = 1.0 / jnp.sqrt(col_top + epsilon)
    for sweep in range(1, PASSES):
        row_top, col_top = row_col_max(rows_of, cols_of, matrix, row_scale, col_scale)
        if sweep == PASSES - 1:
            row_top, need = lax.optimization_barrier((row_top, need))
        row_part, col_top, rest = exchange_max(row_top, col_top)
        if sweep == PASSES - 1:
            row_part, col_top = lax.optimization_barrier((row_part, col_top))
        else:
            row_scale = row_scale / jnp.sqrt(rest(row_part) + epsilon)
        col_scale = col_scale / jnp.sqrt(col_top + epsilon)

    primal_rest = terms = ()
    for k in range(ITERS):
        last = k == ITERS - 1
        primal, ext, drift, weight, *more = primal_update(
            k, obj, cap, col_scale, plan, primal_rest, terms
        )
        if k == 0:
            row_scale = row_scale / jnp.sqrt(rest(row_part) + epsilon)
        pieces = [swap(ext, "rows", o) for o in offsets(row_groups)]
        if k == 0:
            matrix = scale_matrix(rows_of, cols_of, matrix, row_scale, col_scale)
            dual_rest = [need] + [swap(need, "cols", 2 * o) for o in range(1, chips)]
            dual_rest, pieces = lax.optimization_barrier((dual_rest, pieces))
            dual_rest = [row_scale] + dual_rest
        keep, send = forward(rows_of, cols_of, matrix, drift, pieces)
        terms = sum_columns(keep, send)
        outs = dual_update(k, plan, weight, dual_rest, terms, need.shape[1])
        if last:
            dual, packed, weight = outs
            break
        if k == 0:
            demands, outs = outs[0], outs[1:]
        dual, dual_sums, dual_anchors, totals, packed, drift = outs
        primal_rest = (weight, totals, primal, *more)
        dual_rest = (demands, totals, dual, dual_sums, dual_anchors)
        sent = backward(rows_of, cols_of, matrix, packed, swap(packed, "cols", 1), drift)
        terms = [swap(value, "rows", o) for value, o in zip(sent, offsets(row_groups))]

    other = swap(packed, "cols", 1)
    row = lax.broadcasted_iota(jnp.int32, packed.shape, 0)
    total = packed + jnp.where(row == 0, other, 0.0)
    step = 1
    while step < row_groups:
        total = total + swap(total, "rows", step)
        step *= 2
    weight, drift_dual, drift_primal = (
        value[:scenarios] for value in (weight[0], total[0], total[1])
    )
    final = next_weight(weight, restart[-1], drift_dual, drift_primal)
    return (hand_over(primal).T, hand_over(dual).T, final)


def solution(mesh):
    in_specs = (
        P("rows", "cols", None, None, None),
        P("rows", "cols", None),
        P("rows", "cols", None),
        P(("cols", "rows"), None),
        P(("rows", "cols"), None),
        P(("cols", "rows"), None),
        P(),
        P(),
        P(),
    )
    out_specs = (P(("cols", "rows"), None), P(("rows", "cols"), None), P())
    return jax.shard_map(
        on_device, mesh=mesh, in_specs=in_specs, out_specs=out_specs, check_vma=False
    )
```

```python
import functools

import jax
import jax.numpy as jnp
from jax import lax
from jax.experimental import pallas as pl
from jax.experimental.pallas import tpu as pltpu
from jax.sharding import PartitionSpec as P

BLK = 256
RB = 16
CB = 16
PASSES = 3
ITERS = 3
LANES = 128

epsilon = 1e-06
F32 = jnp.float32
BF16 = jnp.bfloat16
VMEM = pl.BlockSpec(memory_space=pltpu.VMEM)
SMEM = pl.BlockSpec(memory_space=pltpu.SMEM)
PARAMS = pltpu.CompilerParams(vmem_limit_bytes=32 * 1024 * 1024)


def offsets(groups):
    return [0] + [o ^ 3 if o < 3 else o for o in range(1, groups)]


def swap(value, axis, offset):
    if offset == 0:
        return value
    count = lax.axis_size(axis)
    return lax.ppermute(value, axis, [(i, i ^ offset) for i in range(count)])


def for_each_block(count, group, body):
    if count == group:
        body(range(count))
    else:

        @pl.loop(0, count // group)
        def _(step):
            body([step * group + k for k in range(group)])


def unit_row(ref, unit):
    row = ref[pl.ds(unit // 2, 1), :]
    return jnp.where(unit % 2 == 0, row[:, :LANES], row[:, LANES:])


def lane_sum(tile):
    return jnp.broadcast_to(jnp.sum(tile, axis=1, keepdims=True), tile.shape)


def split_parts(value):
    parts = []
    for _ in range(3):
        rounded = value.astype(BF16).astype(F32)
        parts.append(rounded)
        value = value - rounded
    return parts


def tail_rows():
    return -(-3 * (lax.axis_size("cols") // 2) // 16) * 16


def to_tail(values, half=0):
    scenarios = values[0][1].shape[0]
    lane = lax.broadcasted_iota(jnp.int32, (scenarios, LANES), 1)
    tile = jnp.zeros((scenarios, LANES), F32)
    for place, value in values:
        for k, part in enumerate(split_parts(value)):
            tile = jnp.where(lane == place + k, part, tile)
    gap = jnp.zeros((LANES // 2 - scenarios, LANES), F32)
    pieces = [jnp.where(half == 0, tile, 0.0), gap, jnp.where(half == 0, 0.0, tile), gap]
    return jnp.concatenate(pieces, axis=0).T[: tail_rows()]


def to_rows(values):
    scenarios = values[0].shape[0]
    lane = lax.broadcasted_iota(jnp.int32, values[0].shape, 1)
    tile = jnp.zeros(values[0].shape, F32)
    for place, value in enumerate(values):
        tile = jnp.where(lane == place, value, tile)
    rest = jnp.zeros((LANES - scenarios, LANES), F32)
    return jnp.concatenate([tile, rest], axis=0).T[:8]


def from_tail(tail, scenarios, first=0, last=LANES):
    rest = jnp.zeros((LANES - tail.shape[0], LANES), F32)
    square = jnp.concatenate([tail, rest], axis=0).T
    tile = square[:scenarios] + square[LANES // 2 : LANES // 2 + scenarios]
    lane = lax.broadcasted_iota(jnp.int32, tile.shape, 1)
    return lane_sum(jnp.where((lane >= first) & (lane < last), tile, 0.0))


def next_weight(weight, restart, drift_dual, drift_primal):
    candidate = jnp.sqrt(
        weight * jnp.sqrt((drift_dual + epsilon) / (drift_primal + epsilon))
    )
    return jnp.where(restart == 1, candidate, weight)


def first_max_kernel(
    places_vmem, a, row_out, col_out, same, places_ref, sem, racc, cacc
):
    del same
    places = pltpu.make_async_copy(places_vmem, places_ref, sem)
    places.start()
    racc[...] = jnp.zeros_like(racc)
    cacc[...] = jnp.zeros_like(cacc)

    def block(n):
        r, c = places_ref[0, n], places_ref[1, n]
        col = cacc[c]
        for t in range(BLK // 32):
            part = pl.ds(t * 32, 32)
            mag = jnp.abs(a[n, part, :])
            col = jnp.maximum(col, jnp.maximum(mag[:16], mag[16:]))
            racc[r, part, :] = jnp.maximum(
                racc[r, part, :], jnp.maximum(mag[:, :LANES], mag[:, LANES:])
            )
        cacc[c] = col

    places.wait()
    for_each_block(a.shape[0], 4, lambda ns: [block(n) for n in ns])
    for b in range(RB):
        flipped = racc[b].astype(F32).T
        row_out[b : b + 1, :] = jnp.max(flipped, axis=0, keepdims=True)
        col_out[b : b + 1, :] = jnp.max(cacc[b].astype(F32), axis=0, keepdims=True)


def max_kernel(
    rows_ref, cols_ref, a, r_ref, c_ref, row_out, col_out, rb, racc, cacc
):
    racc[...] = jnp.zeros_like(racc)
    cacc[...] = jnp.zeros_like(cacc)
    spread_rows(r_ref, rb)

    def block(n):
        r, c = rows_ref[n], cols_ref[n]
        factor = c_ref[pl.ds(c, 1), :]
        col = cacc[c]
        for t in range(BLK // 32):
            part = pl.ds(t * 32, 32)
            mag = jnp.abs(a[n, part, :].astype(F32))
            tall = rb[r, part, :]
            by_row = jnp.concatenate([mag[:, :LANES] * tall, mag[:, LANES:] * tall], 1)
            by_col = mag * factor
            for q in range(4):
                col = jnp.maximum(col, by_row[8 * q : 8 * q + 8])
            racc[r, part, :] = jnp.maximum(
                racc[r, part, :], jnp.maximum(by_col[:, :LANES], by_col[:, LANES:])
            )
        cacc[c] = col

    for_each_block(a.shape[0], 2, lambda ns: [block(n) for n in ns])
    for b in range(RB):
        row_out[b : b + 1, :] = (
            jnp.max(racc[b].T, axis=0, keepdims=True) * r_ref[b : b + 1, :]
        )
        col_out[b : b + 1, :] = (
            jnp.max(cacc[b], axis=0, keepdims=True) * c_ref[b : b + 1, :]
        )


def spread_rows(r_ref, rb):
    for b in range(RB):
        rb[b] = jnp.broadcast_to(r_ref[b : b + 1, :], (LANES, BLK)).T


def first_max(places, matrix):
    count = matrix.shape[0]
    return pl.pallas_call(
        first_max_kernel,
        out_shape=(
            jax.ShapeDtypeStruct((RB, BLK), F32),
            jax.ShapeDtypeStruct((CB, BLK), F32),
            jax.ShapeDtypeStruct(matrix.shape, BF16),
        ),
        in_specs=[VMEM, VMEM],
        out_specs=(VMEM, VMEM, VMEM),
        input_output_aliases={1: 2},
        scratch_shapes=[
            pltpu.SMEM((2, count), jnp.int32),
            pltpu.SemaphoreType.DMA,
            pltpu.VMEM((RB, BLK, LANES), BF16),
            pltpu.VMEM((CB, 16, BLK), BF16),
        ],
        compiler_params=PARAMS,
        name="first_max",
    )(places, matrix)


def row_col_max(rows_of, cols_of, matrix, row_scale, col_scale):
    return pl.pallas_call(
        max_kernel,
        out_shape=(
            jax.ShapeDtypeStruct((RB, BLK), F32),
            jax.ShapeDtypeStruct((CB, BLK), F32),
        ),
        in_specs=[SMEM, SMEM, VMEM, VMEM, VMEM],
        out_specs=(VMEM, VMEM),
        scratch_shapes=[
            pltpu.VMEM((RB, BLK, LANES), F32),
            pltpu.VMEM((RB, BLK, LANES), F32),
            pltpu.VMEM((CB, 8, BLK), F32),
        ],
        compiler_params=PARAMS,
        name="row_col_max",
    )(rows_of, cols_of, matrix, row_scale, col_scale)


def unlike(step, last=False):
    return step if step == 1 or last else step + 1


def exchange_max(row_part, col_part, last=False):
    row_step, col_step = 1, 1
    while col_step < lax.axis_size("rows"):
        row_next = swap(row_part, "cols", unlike(row_step, last))
        col_next = swap(col_part, "rows", col_step)
        row_part = jnp.maximum(row_part, row_next)
        col_part = jnp.maximum(col_part, col_next)
        row_step, col_step = 2 * row_step, 2 * col_step

    def rest(part):
        step = row_step
        while step < lax.axis_size("cols"):
            part = jnp.maximum(part, swap(part, "cols", unlike(step, last)))
            step *= 2
        return part

    return row_part, col_part, rest


def fetch_units(ref, first, count):
    return jnp.concatenate([ref[first + k] for k in range(count)], axis=1)


def scale_kernel(rows_ref, cols_ref, a, r_ref, c_ref, m, flipped, rb):
    spread_rows(r_ref, rb)

    def block(n):
        r, c = rows_ref[n], cols_ref[n]
        factor = c_ref[pl.ds(c, 1), :]
        for t in range(BLK // 32):
            part = pl.ds(t * 32, 32)
            raw = a[n, part, :].astype(F32)
            tall = rb[r, part, :]
            for half in range(2):
                lanes = slice(half * LANES, (half + 1) * LANES)
                scaled = raw[:, lanes] * tall * factor[:, lanes]
                m[n, part, pl.ds(half * LANES, LANES)] = scaled.astype(BF16)
        flipped[n] = m[n].T

    for_each_block(m.shape[0], 2, lambda ns: [block(n) for n in ns])


def scale_matrix(rows_of, cols_of, matrix, row_scale, col_scale):
    return pl.pallas_call(
        scale_kernel,
        out_shape=[jax.ShapeDtypeStruct(matrix.shape, BF16)] * 2,
        in_specs=[SMEM, SMEM, VMEM, VMEM, VMEM],
        out_specs=[VMEM] * 2,
        scratch_shapes=[pltpu.VMEM((RB, BLK, LANES), F32)],
        compiler_params=PARAMS,
        name="scale_matrix",
    )(rows_of, cols_of, matrix, row_scale, col_scale)


def product_scratch(scenarios):
    return [
        pltpu.VMEM((CB * BLK // LANES, scenarios, LANES), BF16),
        pltpu.VMEM((RB * BLK // LANES, scenarios, LANES), F32),
    ]


def block_products(ns, sources, targets, x, m, acc, dims):
    products = [
        lax.dot_general(
            fetch_units(x, 2 * sources[n], 2), m[n], dims, preferred_element_type=F32
        )
        for n in ns
    ]
    for n, product in zip(ns, products):
        unit = 2 * targets[n]
        acc[unit] += product[:, :LANES]
        acc[unit + 1] += product[:, LANES:]


def forward_kernel(pieces, *refs):
    rows_ref, cols_ref, m, drift = refs[:4]
    piece_refs = refs[4 : 4 + pieces]
    keep, send, x, acc = refs[4 + pieces :]
    scenarios = x.shape[1]
    me = lax.axis_index("rows")
    units = x.shape[0] // pieces
    for o, piece in zip(offsets(pieces), piece_refs):
        for k in range(units):
            x[(me ^ o) * units + k] = piece[k * scenarios : (k + 1) * scenarios, :]
    acc[...] = jnp.zeros_like(acc)
    count = m.shape[0]
    dims = (((1,), (0,)), ((), ()))
    for_each_block(
        count, count, lambda ns: block_products(ns, cols_ref, rows_ref, x, m, acc, dims)
    )
    me, core = lax.axis_index("cols") // 2, lax.axis_index("cols") % 2
    shards = lax.axis_size("cols")
    units = acc.shape[0] // shards
    for chip in range(shards // 2):
        for k in range(units):
            rows = pl.ds((chip * units + k) * scenarios, scenarios)
            keep[rows, :] = acc[(2 * chip + core) * units + k]
            send[rows, :] = acc[(2 * chip + 1 - core) * units + k].astype(BF16)
    tail = to_tail([(3 * me, lane_sum(drift[...]))], core)
    rows = pl.ds(keep.shape[0] - tail_rows(), tail_rows())
    keep[rows, :] = tail
    send[rows, :] = tail.astype(BF16)


def half_rows(scenarios):
    return RB * BLK // 2 // LANES * scenarios + tail_rows()


def forward(rows_of, cols_of, matrix, drift, pieces):
    scenarios = drift.shape[0]
    rows = half_rows(scenarios)
    return pl.pallas_call(
        functools.partial(forward_kernel, len(pieces)),
        out_shape=[
            jax.ShapeDtypeStruct((rows, LANES), F32),
            jax.ShapeDtypeStruct((rows, LANES), BF16),
        ],
        in_specs=[SMEM, SMEM, VMEM, VMEM] + [VMEM] * len(pieces),
        out_specs=[VMEM] * 2,
        scratch_shapes=product_scratch(scenarios),
        compiler_params=PARAMS,
        name="forward",
    )(rows_of, cols_of, matrix, drift, *pieces)


def backward_kernel(*refs):
    rows_ref, cols_ref, m, own, other, drift, keep = refs[:7]
    sends, (y, acc) = refs[7:-2], refs[-2:]
    scenarios = y.shape[1]
    core = lax.axis_index("cols") % 2
    shards = lax.axis_size("cols")
    units = y.shape[0] // shards
    for half, ref in ((core, own), (1 - core, other)):
        for chip in range(shards // 2):
            for k in range(units):
                start = (chip * units + k) * scenarios
                y[(2 * chip + half) * units + k] = ref[start : start + scenarios, :]
    acc[...] = jnp.zeros_like(acc)
    count = m.shape[0]
    dims = (((1,), (0,)), ((), ()))
    for_each_block(
        count, count, lambda ns: block_products(ns, rows_ref, cols_ref, y, m, acc, dims)
    )
    tail = own[own.shape[0] - tail_rows() :, :].astype(F32)
    tail = tail + other[other.shape[0] - tail_rows() :, :].astype(F32)
    tail = to_tail([(0, from_tail(tail, scenarios)), (3, drift[...])])
    me = lax.axis_index("rows")
    units = acc.shape[0] // (1 + len(sends))
    for o, out in zip(offsets(1 + len(sends)), (keep,) + tuple(sends)):
        for k in range(units):
            out[pl.ds(k * scenarios, scenarios), :] = acc[(me ^ o) * units + k].astype(
                out.dtype
            )
        out[pl.ds(units * scenarios, tail_rows()), :] = tail.astype(out.dtype)


def backward(rows_of, cols_of, matrix, own, other, drift):
    scenarios = drift.shape[0]
    groups = lax.axis_size("rows")
    shape = (CB * BLK // groups // LANES * scenarios + tail_rows(), LANES)
    return pl.pallas_call(
        backward_kernel,
        out_shape=[jax.ShapeDtypeStruct(shape, F32)]
        + [jax.ShapeDtypeStruct(shape, BF16)] * (groups - 1),
        in_specs=[SMEM, SMEM, VMEM, VMEM, VMEM, VMEM],
        out_specs=[VMEM] * groups,
        scratch_shapes=product_scratch(scenarios),
        compiler_params=PARAMS,
        name="backward",
    )(rows_of, cols_of, matrix, own, other, drift)


def settle(again, stride, totals, new, total, anchor):
    total = total + stride * new
    mean = total / totals
    move = mean - anchor
    return (
        jnp.where(again, mean, new),
        jnp.where(again, 0.0, total),
        jnp.where(again, mean, anchor),
        move * move,
    )


def plan_kernel(steps, restarts, weight, out, square):
    square[...] = jnp.zeros_like(square)
    count, scenarios = steps.shape
    square[:count, :scenarios] = steps[...]
    square[count : 2 * count, :scenarios] = restarts[...].astype(F32)
    square[2 * count : 2 * count + 1, :scenarios] = weight[...]
    out[...] = square[...].T[:scenarios]


def make_plan(steps, restarts, weight):
    return pl.pallas_call(
        plan_kernel,
        out_shape=jax.ShapeDtypeStruct((steps.shape[1], LANES), F32),
        in_specs=[VMEM] * 3,
        out_specs=VMEM,
        scratch_shapes=[pltpu.VMEM((LANES, LANES), F32)],
        compiler_params=PARAMS,
        name="make_plan",
    )(steps, restarts, weight)


def column(ref, lane):
    return jnp.broadcast_to(ref[:, lane : lane + 1], (ref.shape[0], LANES))


def primal_kernel(k, terms, *refs):
    first, last = k == 0, k == ITERS - 1
    obj, cap, c_ref, plan = refs[:4]
    refs = refs[4:]
    if not first:
        weight_ref, wt_ref, state, sums, anchors = refs[:5]
        term_refs = refs[5 : 5 + terms]
        refs = refs[5 + terms :]
    state_out, ext, drift, weight_out = refs[:4]
    width = obj.shape[1]
    stride = column(plan, k)
    again = column(plan, ITERS + k) == 1
    if first:
        totals, weight = stride, column(plan, 2 * ITERS)
    else:
        totals, weight = wt_ref[...] + stride, weight_ref[...]
        scenarios = weight.shape[0]
        tail = sum(ref[ref.shape[0] - tail_rows() :, :].astype(F32) for ref in term_refs)
        drift_dual = from_tail(tail, scenarios, 0, 3)
        drift_primal = from_tail(tail, scenarios, 3, 6)
        weight = next_weight(weight, column(plan, ITERS + k - 1), drift_dual, drift_primal)
    weight_out[...] = weight
    step = stride / weight
    place = lax.axis_index("rows")
    units = width // LANES
    moved = jnp.zeros_like(weight)
    for u in range(units):
        span = pl.ds(u * LANES, LANES)
        scale = unit_row(c_ref, place * units + u)
        gradient = obj[:, span] * scale
        upper = cap[:, span] / scale
        if first:
            old = total = anchor = jnp.zeros_like(gradient)
        else:
            old, total, anchor = state[:, span], sums[:, span], anchors[:, span]
            rows = pl.ds(u * obj.shape[0], obj.shape[0])
            product = sum(ref[rows, :].astype(F32) for ref in term_refs)
            gradient = gradient - product
        new = jnp.minimum(jnp.maximum(old - step * gradient, 0.0), upper)
        ext[pl.ds(u * obj.shape[0], obj.shape[0]), :] = (2.0 * new - old).astype(BF16)
        new, total, anchor, square = settle(again, stride, totals, new, total, anchor)
        state_out[:, span] = new
        if not last:
            sums_out, anchors_out = refs[4:]
            sums_out[:, span] = total
            anchors_out[:, span] = anchor
        moved = moved + square
    drift[...] = moved


def primal_update(k, obj, cap, col_scale, plan, rest, terms):
    shape = obj.shape
    tile = jax.ShapeDtypeStruct((shape[0], LANES), F32)
    whole = jax.ShapeDtypeStruct(shape, F32)
    ext = jax.ShapeDtypeStruct((shape[1] // LANES * shape[0], LANES), BF16)
    operands = (obj, cap, col_scale, plan) + tuple(rest) + tuple(terms)
    last = k == ITERS - 1
    return pl.pallas_call(
        functools.partial(primal_kernel, k, len(terms)),
        out_shape=[whole, ext, tile, tile] + [whole] * (0 if last else 2),
        in_specs=[VMEM] * len(operands),
        out_specs=[VMEM] * (4 if last else 6),
        compiler_params=PARAMS,
        name="primal_update",
    )(*operands)


def dual_kernel(iteration, chips, *refs):
    first, last = iteration == 0, iteration == ITERS - 1
    plan, weight_ref = refs[:2]
    refs = refs[2:]
    if first:
        r_ref, refs = refs[0], refs[1:]
        demands, refs = refs[:chips], refs[chips:]
    else:
        need, wt_ref, state, sums, anchors = refs[:5]
        refs = refs[5:]
    parts, refs = (refs[:2], refs[2:4]), refs[4:]
    if last:
        out, drifts, weights, state_out = refs
    else:
        if first:
            need, refs = refs[0], refs[1:]
        state_out, sums_out, anchors_out, wt_out, packed, drift_out = refs
    stride = column(plan, iteration)
    scenarios = stride.shape[0]
    again = column(plan, ITERS + iteration) == 1
    totals = stride if first else wt_ref[...] + stride
    step = stride * weight_ref[...]
    place = lax.axis_index("cols")
    me, core = place // 2, place % 2
    count = state_out.shape[0] // scenarios
    units = count // chips
    if first:
        for o, demand in enumerate(demands):
            for k in range(units):
                scale = unit_row(r_ref, (2 * (me ^ o) + core) * units + k)
                start = pl.multiple_of(((me ^ o) * units + k) * scenarios, 8)
                need[pl.ds(start, scenarios), :] = (
                    demand[:, k * LANES : (k + 1) * LANES] * scale
                )
    moved = jnp.zeros_like(step)
    for k in range(count):
        span = pl.ds(k * scenarios, scenarios)
        part, place = divmod(k, count // 2)
        rows = pl.ds(place * scenarios, scenarios)
        image = sum(ref[rows, :].astype(F32) for ref in parts[part])
        if first:
            old = total = anchor = jnp.zeros_like(image)
        else:
            old, total, anchor = state[span, :], sums[span, :], anchors[span, :]
        new = old + step * (need[span, :] - image)
        new, total, anchor, square = settle(again, stride, totals, new, total, anchor)
        state_out[span, :] = new
        if not last:
            sums_out[span, :] = total
            anchors_out[span, :] = anchor
            packed[span, :] = new.astype(BF16)
        moved = moved + square
    start = count // 2 * scenarios
    tail = sum(ref[start:, :].astype(F32) for ref in parts[1])
    dual, primal = lane_sum(moved), from_tail(tail, scenarios)
    if last:
        drifts[...] = to_rows([dual, primal])
        weights[...] = to_rows([weight_ref[...]])
        for k in range(units):
            start = pl.multiple_of((me * units + k) * scenarios, 8)
            out[:, k * LANES : (k + 1) * LANES] = state_out[pl.ds(start, scenarios), :]
    else:
        wt_out[...] = jnp.where(again, 0.0, totals)
        packed[pl.ds(count * scenarios, tail_rows()), :] = to_tail([(0, dual)], core).astype(BF16)
        drift_out[...] = primal


def dual_update(iteration, plan, weight, rest, terms, width):
    first, last = iteration == 0, iteration == ITERS - 1
    chips = lax.axis_size("cols") // 2
    scenarios = plan.shape[0]
    rows = half_rows(scenarios)
    tile = jax.ShapeDtypeStruct((scenarios, LANES), F32)
    half = jax.ShapeDtypeStruct((rows - tail_rows(), LANES), F32)
    operands = (plan, weight) + tuple(rest) + tuple(terms)
    scratch = []
    if last:
        rows = jax.ShapeDtypeStruct((8, LANES), F32)
        out_shape = [jax.ShapeDtypeStruct((scenarios, width), F32), rows, rows]
        scratch = [pltpu.VMEM(half.shape, F32)]
    else:
        packed = jax.ShapeDtypeStruct((rows, LANES), BF16)
        out_shape = [half] * (3 + first) + [tile, packed, tile]
    return pl.pallas_call(
        functools.partial(dual_kernel, iteration, chips),
        out_shape=out_shape,
        in_specs=[VMEM] * len(operands),
        out_specs=[VMEM] * len(out_shape),
        scratch_shapes=scratch,
        compiler_params=PARAMS,
        name="dual_update",
    )(*operands)


def copy_kernel(source, out):
    out[...] = source[...]


def hand_over(value):
    return pl.pallas_call(
        copy_kernel,
        out_shape=jax.ShapeDtypeStruct(value.shape, value.dtype),
        in_specs=[VMEM],
        out_specs=VMEM,
        compiler_params=PARAMS,
        name="hand_over",
    )(value)


def sum_columns(keep, send):
    chips = lax.axis_size("cols") // 2
    joined = keep + swap(send, "cols", 1).astype(F32)
    middle = (joined.shape[0] - tail_rows()) // 2
    parts = [joined[:middle], joined[middle:]]
    steps = [1 << k for k in range(chips.bit_length() - 1)]
    for k in range(len(steps)):
        got = [
            swap(part.astype(BF16), "cols", 2 * order[k])
            for part, order in zip(parts, (steps, steps[::-1]))
        ]
        if k == len(steps) - 1:
            return [parts[0], got[0], parts[1], got[1]]
        parts = [part + more.astype(F32) for part, more in zip(parts, got)]


def on_device(
    blocks, block_row, block_col, objective, demand, capacity, step_size, restart, primal_weight
):
    rows_of = block_row[0, 0]
    cols_of = block_col[0, 0]
    chips = lax.axis_size("cols") // 2
    row_groups = lax.axis_size("rows")
    scenarios = objective.shape[1]
    obj, cap, need = objective.T, capacity.T, demand.T
    plan = make_plan(step_size, restart, primal_weight[None])

    matrix = blocks[0, 0]
    row_top, col_top, matrix = first_max(jnp.stack([rows_of, cols_of]), matrix)
    row_part, col_top, rest = exchange_max(row_top, col_top)
    row_scale = 1.0 / jnp.sqrt(rest(row_part) + epsilon)
    col_scale = 1.0 / jnp.sqrt(col_top + epsilon)
    for sweep in range(1, PASSES):
        row_top, col_top = row_col_max(rows_of, cols_of, matrix, row_scale, col_scale)
        if sweep == PASSES - 1:
            row_top, need = lax.optimization_barrier((row_top, need))
        row_part, col_top, rest = exchange_max(row_top, col_top, sweep == PASSES - 1)
        if sweep == PASSES - 1:
            row_part, col_top = lax.optimization_barrier((row_part, col_top))
        else:
            row_scale = row_scale / jnp.sqrt(rest(row_part) + epsilon)
        col_scale = col_scale / jnp.sqrt(col_top + epsilon)

    primal_rest = terms = ()
    for k in range(ITERS):
        last = k == ITERS - 1
        primal, ext, drift, weight, *more = primal_update(
            k, obj, cap, col_scale, plan, primal_rest, terms
        )
        if k == 0:
            row_scale = row_scale / jnp.sqrt(rest(row_part) + epsilon)
        pieces = [swap(ext, "rows", o) for o in offsets(row_groups)]
        if k == 0:
            matrix, flipped = scale_matrix(rows_of, cols_of, matrix, row_scale, col_scale)
            dual_rest = [need] + [swap(need, "cols", 2 * o) for o in range(1, chips)]
            dual_rest, pieces = lax.optimization_barrier((dual_rest, pieces))
            dual_rest = [row_scale] + dual_rest
        keep, send = forward(rows_of, cols_of, flipped, drift, pieces)
        terms = sum_columns(keep, send)
        outs = dual_update(k, plan, weight, dual_rest, terms, need.shape[1])
        if last:
            dual, packed, weight = outs
            break
        if k == 0:
            demands, outs = outs[0], outs[1:]
        dual, dual_sums, dual_anchors, totals, packed, drift = outs
        primal_rest = (weight, totals, primal, *more)
        dual_rest = (demands, totals, dual, dual_sums, dual_anchors)
        sent = backward(rows_of, cols_of, matrix, packed, swap(packed, "cols", 1), drift)
        terms = [swap(value, "rows", o) for value, o in zip(sent, offsets(row_groups))]

    other = swap(packed, "cols", 1)
    row = lax.broadcasted_iota(jnp.int32, packed.shape, 0)
    total = packed + jnp.where(row == 0, other, 0.0)
    step = 1
    while step < row_groups:
        total = total + swap(total, "rows", step)
        step *= 2
    weight, drift_dual, drift_primal = (
        value[:scenarios] for value in (weight[0], total[0], total[1])
    )
    final = next_weight(weight, restart[-1], drift_dual, drift_primal)
    return (hand_over(primal).T, hand_over(dual).T, final)


def solution(mesh):
    in_specs = (
        P("rows", "cols", None, None, None),
        P("rows", "cols", None),
        P("rows", "cols", None),
        P(("cols", "rows"), None),
        P(("rows", "cols"), None),
        P(("cols", "rows"), None),
        P(),
        P(),
        P(),
    )
    out_specs = (P(("cols", "rows"), None), P(("rows", "cols"), None), P())
    return jax.shard_map(
        on_device, mesh=mesh, in_specs=in_specs, out_specs=out_specs, check_vma=False
    )
```
